32 devices in a mesh: groups: 2 (over y), fsdp: 4 (over z), dp: 2 (over x), rep: 2 (over core).
Axes of the slice: x: 2, y: 2, z: 4, core: 2. Of those that a mesh axis runs over, the one named last changes fastest.
Arguments:
- hidden_in: bfloat16 [8, 2048, 8192], P(('groups', 'dp'), 'rep', 'fsdp'), parts along dimension 0, may hold values from -6 to 6
- query_grad: bfloat16 [8, 2048, 8192], P(('groups', 'dp'), 'rep', 'fsdp'), parts along dimension 0, may hold values from -6 to 6
- value_grad: bfloat16 [8, 2048, 1024], P(('groups', 'dp'), 'rep', 'fsdp'), parts along dimension 0, may hold values from -6 to 6
- query_down: bfloat16 [8192, 64], P('fsdp'), may hold values from -0.0625 to 0.0625
- query_up: bfloat16 [64, 8192], P(None, 'fsdp'), may hold values from -0.0625 to 0.0625
- value_down: bfloat16 [8192, 64], P('fsdp'), may hold values from -0.0625 to 0.0625
- value_up: bfloat16 [64, 1024], P(None, 'fsdp'), may hold values from -0.1875 to 0.1875
- lengths: int32 [8], P(('groups', 'dp')), parts along dimension 0, may hold values from 1 to 2048, 4100 in all
- owners: int32 [8], P('groups'), parts along dimension 0, may hold values from 0 to 3, each once
- proj_seed: int32 [1], replicated, may hold values from 0 to 999999
- offsets: int32 [7], replicated, may hold values from 0 to 1048575
Outputs:
- projected: float32 [8, 8192], P(('groups', 'dp'), ('fsdp', 'rep')), parts along dimension 0
The draws below stay inside these ranges and needn't reach their ends.
There are 2 independent parts, one for each index of `groups`. The reference program is written for one: setup_inputs(seed, part) draws one part's arguments, and reference() takes and returns one part's arrays. A program takes and returns all parts, laid end to end along the dimension named above; an argument that names none is the same for every part. Nothing has to cross between parts.
Inputs may be any that keep to these rules, and one draw needn't show every extreme that they name: `lengths`: every example has at least one live position, and some example has 2048; the total given with the table holds within each group's 4 examples, not over the groups together. owners names every row once.
All inputs are finite; a program needn't handle non-finite values.
Results may differ from the reference program's by a relative error of at most 0.0003.
Values sent between devices are 32-bit elements; how exact they have to be, the bound alone decides.
No kernel may reach another device: no remote copies, remote signals or barrier semaphores. Data moves between devices by JAX's collectives and lax.ppermute only.
A program may use at most 128 MiB of HBM per device.

```python
import math
import jax
import jax.numpy as jnp
import numpy as np
from jax import lax

D = 8192
DQ = 8192
DV = 1024
R = 64
KP = 512
KR = 4
LMAX = 2048
FEAT = 8192
EXAMPLES = 4


def set_ends(array, stream_key, least, largest):
    place = [jax.random.randint(jax.random.fold_in(stream_key, axis), (), 0, length) for axis, length in enumerate(array.shape)]
    main_axis = array.shape.index(max(array.shape))
    beside = place[:main_axis] + [(place[main_axis] + 1) % array.shape[main_axis]] + place[main_axis + 1:]
    return array.at[tuple(place)].set(least).at[tuple(beside)].set(largest)


def steps_of(stream_key, extent, shards, low, top_value):
    def one(dim, blocks):
        steps = jax.random.uniform(jax.random.fold_in(jax.random.fold_in(stream_key, 6), dim), (blocks,), jnp.float32, low / len(shards), top_value / len(shards))
        return jnp.repeat(jnp.exp(steps), extent[dim] // blocks).reshape((-1,) + (1,) * (len(extent) - dim - 1))

    loudness = one(*shards[0])
    for cut in shards[1:]:
        loudness = loudness * one(*cut)
    return loudness


def length_profile(count, total, reach, lean):
    weights = [(1 << 20) // math.isqrt(rank ** lean) + 1 for rank in range(2, count + 1)]
    rest, given = total - reach - (count - 1), [1] * (count - 1)
    while rest > 0:
        free = [i for i in range(count - 1) if given[i] < reach]
        mass, budget = sum([weights[i] for i in free]), rest
        for i in free:
            addition = min(reach - given[i], max(1, budget * weights[i] // mass), rest)
            given[i] = given[i] + addition
            rest = rest - addition
    return np.array([reach] + given)


def ragged(own_key, number_of, total, reach, lean):
    if number_of == 2:
        one = jax.random.randint(own_key, (), max(1, total - reach), min(reach, total - 1) + 1)
        return jnp.stack([one, total - one])
    tallies = jnp.asarray(length_profile(number_of, total, reach, lean), jnp.int32)
    twos = (number_of - 1) // 2
    donor, taker = tallies[1:1 + 2 * twos:2], tallies[2:2 + 2 * twos:2]
    margin = jnp.minimum(donor - 1, reach - taker)
    shifted = jax.random.randint(jax.random.fold_in(own_key, 1), (twos,), 0, 1 << 20) % (margin + 1)
    tallies = tallies.at[1:1 + 2 * twos:2].set(donor - shifted).at[2:2 + 2 * twos:2].set(taker + shifted)
    return tallies[jax.random.permutation(jax.random.fold_in(own_key, 2), number_of)]


def bell_draw(rng, extent, scale, limit, shards=(), held_as=jnp.bfloat16):
    gain = steps_of(rng, extent, shards, -0.22, 0.18) if shards else 1.0
    array = jax.random.normal(rng, extent, jnp.float32) * scale * gain
    return jnp.minimum(jnp.maximum(array, -limit), limit).astype(held_as)


def setup_inputs(seed: int = 0, part: int = 0) -> dict:
    keys = jax.random.split(jax.random.key(seed), 12)
    part_keys = jax.random.split(jax.random.fold_in(keys[11], part), 12)
    return {
        "hidden_in": bell_draw(part_keys[0], (EXAMPLES, LMAX, D), 1.0, 6.0, ((0, 2), (1, 2), (2, 4))),
        "query_grad": bell_draw(part_keys[1], (EXAMPLES, LMAX, DQ), 1.0, 6.0, ((0, 2), (1, 2), (2, 4))),
        "value_grad": bell_draw(part_keys[2], (EXAMPLES, LMAX, DV), 1.0, 6.0, ((0, 2), (1, 2), (2, 4))),
        "query_down": bell_draw(keys[3], (D, R), D ** -0.5, 0.0625, ((0, 4),)),
        "query_up": bell_draw(keys[4], (R, DQ), DQ ** -0.5, 0.0625, ((1, 4),)),
        "value_down": bell_draw(keys[5], (D, R), D ** -0.5, 0.0625, ((0, 4),)),
        "value_up": bell_draw(keys[6], (R, DV), DV ** -0.5, 0.1875, ((1, 4),)),
        "lengths": ragged(part_keys[7], EXAMPLES, EXAMPLES * LMAX // 2 + EXAMPLES, LMAX, 2).astype(jnp.int32),
        "owners": jax.random.permutation(part_keys[8], EXAMPLES).astype(jnp.int32),
        "proj_seed": jax.random.randint(keys[9], (1,), 0, 1000000).astype(jnp.int32),
        "offsets": set_ends(jax.random.randint(keys[10], (7,), 0, 1048576), jax.random.fold_in(keys[10], 1), 0, 1048575).astype(jnp.int32),
    }


def mix_bits(values):
    values = values ^ ((values >> 15) & 131071)
    values = values * -2048144777
    values = values ^ ((values >> 13) & 524287)
    values = values * -1028477379
    values = values ^ ((values >> 16) & 65535)
    return values


def table_block(seed_value, offset, row_start, rows, cols):
    row_index = lax.broadcasted_iota(jnp.int32, (rows, cols), 0) + row_start
    col_index = lax.broadcasted_iota(jnp.int32, (rows, cols), 1)
    counter = offset + row_index * cols + col_index
    hashed = mix_bits(counter * -1640531535 + seed_value * 668265263)
    levels = (hashed & 255).astype(jnp.float32)
    return ((levels - 127.5) / 128.0).astype(jnp.bfloat16)


def reference(hidden_in, query_grad, value_grad, query_down, query_up, value_down, value_up, lengths, owners, proj_seed, offsets):
    seed_value = proj_seed[0]
    wide_in = table_block(seed_value, offsets[0], 0, D, KP)
    wide_query = table_block(seed_value, offsets[1], 0, DQ, KP)
    wide_value = table_block(seed_value, offsets[2], 0, DV, KP)
    rank_tables = [table_block(seed_value, offsets[3 + k], 0, R, KR).astype(jnp.float32) for k in range(4)]
    rank_scale = (R / 3.0) ** -0.5
    high = lax.Precision.HIGHEST

    def one_example(items):
        tokens, qgrad, vgrad, length = items
        positions = lax.broadcasted_iota(jnp.int32, (LMAX, 1), 0)
        mask = (positions < length).astype(jnp.float32)
        down_q = jnp.dot(tokens, query_down, preferred_element_type=jnp.float32)
        up_q = jnp.dot(qgrad, query_up.T, preferred_element_type=jnp.float32)
        down_v = jnp.dot(tokens, value_down, preferred_element_type=jnp.float32)
        up_v = jnp.dot(vgrad, value_up.T, preferred_element_type=jnp.float32)
        sides = [jnp.dot(part, table, precision=high) * rank_scale * mask
                 for part, table in zip([up_q, up_v, down_q, down_v], rank_tables)]
        wide_x = jnp.dot(tokens, wide_in, preferred_element_type=jnp.float32) * (D / 3.0) ** -0.5
        wide_q = jnp.dot(qgrad, wide_query, preferred_element_type=jnp.float32) * (DQ / 3.0) ** -0.5
        wide_v = jnp.dot(vgrad, wide_value, preferred_element_type=jnp.float32) * (DV / 3.0) ** -0.5
        blocks = [jnp.dot(wide_x.T, sides[0], precision=high),
                  jnp.dot(wide_x.T, sides[1], precision=high),
                  jnp.dot(wide_q.T, sides[2], precision=high),
                  jnp.dot(wide_v.T, sides[3], precision=high)]
        return jnp.stack(blocks).reshape(FEAT) * LMAX ** -0.5

    feats = lax.map(one_example, (hidden_in, query_grad, value_grad, lengths))
    projected = jnp.zeros((EXAMPLES, FEAT), jnp.float32).at[owners].set(feats)
    return projected
```

```python
import functools

import jax
import jax.numpy as jnp
from jax import lax
from jax.experimental import pallas as pl
from jax.experimental.pallas import tpu as pltpu
from jax.sharding import PartitionSpec as P

D = 8192
DQ = 8192
DV = 1024
R = 64
KP = 512
KR = 4
LMAX = 2048
BLOCK = 256
SEED_MUL = 668265263
COUNT_MUL = -1640531535
BF16 = jnp.bfloat16
F32 = jnp.float32
SCALARS = 24


def mix_bits(values):
    values = values ^ lax.shift_right_logical(values, 15)
    values = values * -2048144777
    values = values ^ lax.shift_right_logical(values, 13)
    values = values * -1028477379
    return values ^ lax.shift_right_logical(values, 16)


def wrapped(value):
    return (value + 2**31) % 2**32 - 2**31


def centred(counter_hash):
    return (mix_bits(counter_hash) & 255).astype(F32) - 127.5


def split_rows(values):
    high = values.astype(BF16).astype(F32)
    return jnp.concatenate([high, values - high], axis=0).astype(BF16)


def join_rows(product):
    half = product.shape[0] // 2
    return product[:half] + product[half:]


def rank_rows(seed_value, offset, first):
    row = lax.broadcasted_iota(jnp.int32, (2 * KR, R), 0) - first
    col = lax.broadcasted_iota(jnp.int32, (2 * KR, R), 1)
    counter = offset + col * KR + row
    entry = centred(counter * COUNT_MUL + seed_value * SEED_MUL)
    return jnp.where((row >= 0) & (row < KR), entry, 0.0).astype(BF16)


def side_kernel(
    hidden_hbm,
    query_hbm,
    value_hbm,
    query_down_hbm,
    query_up_hbm,
    value_down_hbm,
    value_up_hbm,
    lengths_hbm,
    seed_hbm,
    offsets_hbm,
    side_ref,
    hidden_ref,
    query_ref,
    value_ref,
    query_down,
    query_up,
    value_down,
    value_up,
    lengths,
    seed,
    offsets,
    block_sem,
    factor_sem,
    scalar_sem,
):
    count, rows, _ = hidden_ref.shape
    blocks = rows // BLOCK
    start = lax.axis_index("rep") * rows
    scalars = [
        pltpu.make_async_copy(src, dst, scalar_sem.at[k])
        for k, (src, dst) in enumerate(
            ((lengths_hbm, lengths), (seed_hbm, seed), (offsets_hbm, offsets))
        )
    ]
    factors = [
        pltpu.make_async_copy(src, dst, factor_sem.at[k])
        for k, (src, dst) in enumerate(
            (
                (query_up_hbm, query_up),
                (value_up_hbm, value_up),
                (query_down_hbm, query_down),
                (value_down_hbm, value_down),
            )
        )
    ]
    for copy in scalars + factors:
        copy.start()
    arrays = ((query_hbm, query_ref), (value_hbm, value_ref), (hidden_hbm, hidden_ref))
    copies = [
        [
            [
                pltpu.make_async_copy(
                    src.at[item, pl.ds(block * BLOCK, BLOCK)],
                    dst.at[item, pl.ds(block * BLOCK, BLOCK)],
                    block_sem.at[k, item, block],
                )
                for block in range(blocks)
            ]
            for item in range(count)
        ]
        for k, (src, dst) in enumerate(arrays)
    ]
    scalars[0].wait()
    for per_array in copies:
        for item in range(count):
            for block in range(blocks):

                @pl.when(start + block * BLOCK < lengths[item])
                def _(copy=per_array[item][block]):
                    copy.start()

    for copy in scalars[1:] + factors:
        copy.wait()
    seed_value = seed[0]

    def up_map(factor, k, first):
        table = rank_rows(seed_value, offsets[3 + k], first)
        return jnp.dot(table, factor[...], preferred_element_type=F32)

    def down_map(factor, k, first):
        table = rank_rows(seed_value, offsets[3 + k], first)
        return lax.dot_general(
            table, factor[...], (((1,), (1,)), ((), ())), preferred_element_type=F32
        )

    from_query = split_rows(up_map(query_up, 0, 0))
    from_value = split_rows(up_map(value_up, 1, KR))
    from_hidden = split_rows(down_map(query_down, 2, 0) + down_map(value_down, 3, KR))

    def project(weights, data):
        product = lax.dot_general(
            weights, data, (((1,), (1,)), ((), ())), preferred_element_type=F32
        )
        return join_rows(product)

    def each_block(visit):
        for item in range(count):
            for block in range(blocks):
                live = start + block * BLOCK < lengths[item]
                visit(item, block, pl.ds(block * BLOCK, BLOCK), pl.ds(item * rows + block * BLOCK, BLOCK), live)

    def keep(item, block):
        position = lax.broadcasted_iota(jnp.int32, (2 * KR, BLOCK), 1)
        return position + (start + block * BLOCK) < lengths[item]

    def upper(item, block, here, out, live):
        @pl.when(live)
        def _():
            copies[0][item][block].wait()
            copies[1][item][block].wait()
            rows_ = project(from_query, query_ref[item, here, :])
            rows_ = rows_ + project(from_value, value_ref[item, here, :])
            side_ref[: 2 * KR, out] = jnp.where(keep(item, block), rows_, 0.0)

        @pl.when(jnp.logical_not(live))
        def _():
            side_ref[: 2 * KR, out] = jnp.zeros((2 * KR, BLOCK), F32)
            query_ref[item, here, :] = jnp.zeros((BLOCK, query_ref.shape[2]), BF16)
            value_ref[item, here, :] = jnp.zeros((BLOCK, value_ref.shape[2]), BF16)

    def lower(item, block, here, out, live):
        @pl.when(live)
        def _():
            copies[2][item][block].wait()
            rows_ = project(from_hidden, hidden_ref[item, here, :])
            side_ref[2 * KR :, out] = jnp.where(keep(item, block), rows_, 0.0)

        @pl.when(jnp.logical_not(live))
        def _():
            side_ref[2 * KR :, out] = jnp.zeros((2 * KR, BLOCK), F32)
            hidden_ref[item, here, :] = jnp.zeros((BLOCK, hidden_ref.shape[2]), BF16)

    each_block(upper)
    each_block(lower)


def table_kernel(step_rows, tables, seed_ref, offsets_ref, _, *outs):
    shard = lax.axis_index("fsdp")
    seed_term = seed_ref[0] * SEED_MUL
    for k, out in zip(tables, outs):
        rows = out.shape[0]
        row = lax.broadcasted_iota(jnp.int32, (step_rows, KP), 0)
        col = lax.broadcasted_iota(jnp.int32, (step_rows, KP), 1)
        counter = offsets_ref[k] + (row + shard * rows) * KP + col
        first = counter * COUNT_MUL + seed_term
        stride = wrapped(step_rows * KP * COUNT_MUL)

        def step(i, values, out=out, stride=stride):
            here = pl.ds(pl.multiple_of(i * step_rows, step_rows), step_rows)
            out[here, :] = centred(values).astype(BF16)
            return values + stride

        lax.fori_loop(0, rows // step_rows, step, first, unroll=4)


def feature_kernel(
    side_ref,
    hidden_ref,
    query_ref,
    value_ref,
    wide_in,
    wide_query,
    wide_value,
    owners_hbm,
    out_ref,
    owners,
    owner_sem,
):
    fetch = pltpu.make_async_copy(owners_hbm, owners, owner_sem)
    fetch.start()
    count, rows, _ = hidden_ref.shape
    half = 2 * KR

    def gathered(data_ref, first):
        parts = []
        for item in range(count):
            side = side_ref[first : first + half, item * rows : (item + 1) * rows]
            product = jnp.dot(split_rows(side), data_ref[item], preferred_element_type=F32)
            parts.append(join_rows(product))
        return jnp.concatenate(parts, axis=0)

    def widened(gathered_rows, table):
        product = jnp.dot(split_rows(gathered_rows), table[...], preferred_element_type=F32)
        return join_rows(product)

    side_scale = (R / 3.0) ** (-0.5) / 128.0 * LMAX ** (-0.5) / 128.0
    upper = widened(gathered(hidden_ref, 0), wide_in) * (side_scale * (D / 3.0) ** (-0.5))
    query = widened(gathered(query_ref, half), wide_query) * (side_scale * (DQ / 3.0) ** (-0.5))
    value = widened(gathered(value_ref, half), wide_value) * (side_scale * (DV / 3.0) ** (-0.5))
    group = lax.rem(lax.broadcasted_iota(jnp.int32, query.shape, 0), half)
    lower = jnp.where(group < KR, query, value)
    fetch.wait()
    first = lax.axis_index("dp") * count
    targets = [owners[first + item] for item in range(count)]
    halves, spots, pieces, slot_rows, width = out_ref.shape
    slots = slot_rows // KR
    chunks = halves * pieces
    per_block = KP // width
    zero = jnp.zeros((KR, KP), F32)
    for spot in range(spots):
        for block in range(4):
            source, at = (upper, lower)[block // 2], (block % 2) * KR
            wanted = []
            for slot in range(slots):
                total = zero
                for item in range(count):
                    rows_ = source[item * half + at : item * half + at + KR]
                    total = total + jnp.where(targets[item] == spot * slots + slot, rows_, 0.0)
                wanted.append(total)
            wanted = jnp.concatenate(wanted, axis=0)
            for part in range(per_block):
                chunk = block * per_block + part
                if chunk < chunks:
                    out_ref[chunk % halves, spot, chunk // halves] = wanted[
                        :, part * width : (part + 1) * width
                    ]


def finish_kernel(pieces_ref, out_ref):
    sources, _, width = pieces_ref.shape
    total = pieces_ref[0]
    for source in range(1, sources):
        total = total + pieces_ref[source]
    high = total.astype(BF16).astype(F32)
    rest = total - high
    middle = rest.astype(BF16).astype(F32)
    parts = jnp.concatenate([high, middle, rest - middle], axis=0).astype(BF16)
    row = lax.broadcasted_iota(jnp.int32, (width, width * KR), 0)
    col = lax.broadcasted_iota(jnp.int32, (width, width * KR), 1)
    spread = jnp.where(lax.shift_right_logical(col, 2) == row, 1.0, 0.0).astype(BF16)
    wide = jnp.dot(parts, spread, preferred_element_type=F32)
    count = total.shape[0]
    wide = wide[:count] + wide[count : 2 * count] + wide[2 * count :]
    rank = lax.broadcasted_iota(jnp.int32, wide.shape, 0) & (KR - 1)
    place = lax.broadcasted_iota(jnp.int32, wide.shape, 1) & (KR - 1)
    wide = jnp.where(rank == place, wide, 0.0)
    for slot in range(out_ref.shape[0]):
        out_ref[slot : slot + 1, :] = jnp.sum(
            wide[slot * KR : (slot + 1) * KR], axis=0, keepdims=True
        )


def in_vmem():
    return pl.BlockSpec(memory_space=pltpu.VMEM)


def anywhere():
    return pl.BlockSpec(memory_space=pl.ANY)


def in_smem():
    return pl.BlockSpec(memory_space=pltpu.SMEM)


def per_device(
    hidden_in,
    query_grad,
    value_grad,
    query_down,
    query_up,
    value_down,
    value_up,
    lengths,
    owners,
    proj_seed,
    offsets,
):
    count, rows, in_cols = hidden_in.shape
    q_cols = query_grad.shape[2]
    v_cols = value_grad.shape[2]
    shards = lax.axis_size("fsdp")
    spots = lax.axis_size("dp")
    halves = lax.axis_size("rep")
    side, hidden, query, value = pl.pallas_call(
        side_kernel,
        out_shape=(
            pltpu.VMEM((4 * KR, count * rows), F32),
            pltpu.VMEM(hidden_in.shape, BF16),
            pltpu.VMEM(query_grad.shape, BF16),
            pltpu.VMEM(value_grad.shape, BF16),
        ),
        in_specs=[anywhere()] * 10,
        out_specs=[in_vmem()] * 4,
        scratch_shapes=[
            pltpu.VMEM(query_down.shape, BF16),
            pltpu.VMEM(query_up.shape, BF16),
            pltpu.VMEM(value_down.shape, BF16),
            pltpu.VMEM(value_up.shape, BF16),
            pltpu.SMEM(lengths.shape, jnp.int32),
            pltpu.SMEM(proj_seed.shape, jnp.int32),
            pltpu.SMEM(offsets.shape, jnp.int32),
            pltpu.SemaphoreType.DMA((3, count, rows // BLOCK)),
            pltpu.SemaphoreType.DMA((4,)),
            pltpu.SemaphoreType.DMA((3,)),
        ],
        compiler_params=pltpu.CompilerParams(vmem_limit_bytes=24 * 2**20),
        name="sides",
    )(
        hidden_in,
        query_grad,
        value_grad,
        query_down,
        query_up,
        value_down,
        value_up,
        lengths,
        proj_seed,
        offsets,
    )

    def make_tables(which, sizes, after):
        return pl.pallas_call(
            functools.partial(table_kernel, 32, which),
            out_shape=[pltpu.VMEM((size, KP), BF16) for size in sizes],
            in_specs=[in_smem(), in_smem(), in_vmem()],
            out_specs=[in_vmem()] * len(sizes),
            compiler_params=pltpu.CompilerParams(vmem_limit_bytes=16 * 2**20),
            name="tables",
        )(proj_seed, offsets, after)

    hop = 1
    stages = [side]
    while hop < shards:
        pairs = [(i, i ^ hop) for i in range(shards)]
        stages.append(stages[-1] + lax.ppermute(stages[-1], "fsdp", pairs))
        hop *= 2
    (wide_in,) = make_tables((0,), (in_cols,), stages[0])
    wide_query, wide_value = make_tables((1, 2), (q_cols, v_cols), stages[1])
    examples = owners.shape[0]
    slots = examples // spots
    width = 4 * KP // (shards * halves)
    pieces = pl.pallas_call(
        feature_kernel,
        out_shape=pltpu.VMEM((halves, spots, shards, slots * KR, width), F32),
        in_specs=[in_vmem()] * 7 + [anywhere()],
        out_specs=in_vmem(),
        scratch_shapes=[pltpu.SMEM(owners.shape, jnp.int32), pltpu.SemaphoreType.DMA],
        compiler_params=pltpu.CompilerParams(vmem_limit_bytes=16 * 2**20),
        name="features",
    )(stages[-1], hidden, query, value, wide_in, wide_query, wide_value, owners)
    half = lax.axis_index("rep")
    kept = lax.dynamic_index_in_dim(pieces, half, 0, keepdims=False)
    sent = lax.dynamic_index_in_dim(pieces, 1 - half, 0, keepdims=False)
    both = kept + lax.ppermute(sent, "rep", [(0, 1), (1, 0)])
    parts = both.reshape(spots * shards, slots * KR, width)
    parts = lax.all_to_all(parts, ("dp", "fsdp"), 0, 0)
    return pl.pallas_call(
        finish_kernel,
        out_shape=jax.ShapeDtypeStruct((slots, width * KR), F32),
        in_specs=[in_vmem()],
        out_specs=in_vmem(),
        compiler_params=pltpu.CompilerParams(vmem_limit_bytes=16 * 2**20),
        name="finish",
    )(parts)


def solution(mesh):
    placed = (
        P(("groups", "dp"), "rep", "fsdp"),
        P(("groups", "dp"), "rep", "fsdp"),
        P(("groups", "dp"), "rep", "fsdp"),
        P("fsdp", None),
        P(None, "fsdp"),
        P("fsdp", None),
        P(None, "fsdp"),
        P(("groups", "dp")),
        P("groups"),
        P(),
        P(),
    )
    return jax.shard_map(
        per_device,
        mesh=mesh,
        in_specs=placed,
        out_specs=P(("groups", "dp"), ("fsdp", "rep")),
        check_vma=False,
    )
```

```python
import functools

import jax
import jax.numpy as jnp
from jax import lax
from jax.experimental import pallas as pl
from jax.experimental.pallas import tpu as pltpu
from jax.sharding import PartitionSpec as P

D = 8192
DQ = 8192
DV = 1024
R = 64
KP = 512
KR = 4
LMAX = 2048
BLOCK = 256
SEED_MUL = 668265263
COUNT_MUL = -1640531535
BF16 = jnp.bfloat16
F32 = jnp.float32


def mix_bits(values):
    values = values ^ lax.shift_right_logical(values, 15)
    values = values * -2048144777
    values = values ^ lax.shift_right_logical(values, 13)
    values = values * -1028477379
    return values ^ lax.shift_right_logical(values, 16)


def wrapped(value):
    return (value + 2**31) % 2**32 - 2**31


def centred(counter_hash):
    return (mix_bits(counter_hash) & 255).astype(F32) - 127.5


def split_rows(values):
    high = values.astype(BF16).astype(F32)
    return jnp.concatenate([high, values - high], axis=0).astype(BF16)


def join_rows(product):
    half = product.shape[0] // 2
    return product[:half] + product[half:]


def rank_rows(seed_value, offset, first):
    row = lax.broadcasted_iota(jnp.int32, (2 * KR, R), 0) - first
    col = lax.broadcasted_iota(jnp.int32, (2 * KR, R), 1)
    counter = offset + col * KR + row
    entry = centred(counter * COUNT_MUL + seed_value * SEED_MUL)
    return jnp.where((row >= 0) & (row < KR), entry, 0.0).astype(BF16)


def side_kernel(
    hidden_hbm,
    query_hbm,
    value_hbm,
    query_down_hbm,
    query_up_hbm,
    value_down_hbm,
    value_up_hbm,
    lengths_hbm,
    seed_hbm,
    offsets_hbm,
    owners_hbm,
    side_ref,
    scalar_ref,
    hidden_ref,
    query_ref,
    value_ref,
    query_down,
    query_up,
    value_down,
    value_up,
    lengths,
    seed,
    offsets,
    owners,
    block_sem,
    factor_sem,
    scalar_sem,
):
    count, rows, _ = hidden_ref.shape
    blocks = rows // BLOCK
    start = lax.axis_index("rep") * rows
    scalars = [
        pltpu.make_async_copy(src, dst, scalar_sem.at[k])
        for k, (src, dst) in enumerate(
            (
                (lengths_hbm, lengths),
                (seed_hbm, seed),
                (offsets_hbm, offsets),
                (owners_hbm, owners),
            )
        )
    ]
    factors = [
        pltpu.make_async_copy(src, dst, factor_sem.at[k])
        for k, (src, dst) in enumerate(
            (
                (query_up_hbm, query_up),
                (value_up_hbm, value_up),
                (query_down_hbm, query_down),
                (value_down_hbm, value_down),
            )
        )
    ]
    for copy in scalars + factors:
        copy.start()
    arrays = ((query_hbm, query_ref), (value_hbm, value_ref), (hidden_hbm, hidden_ref))
    copies = [
        [
            [
                pltpu.make_async_copy(
                    src.at[item, pl.ds(block * BLOCK, BLOCK)],
                    dst.at[item, pl.ds(block * BLOCK, BLOCK)],
                    block_sem.at[k, item, block],
                )
                for block in range(blocks)
            ]
            for item in range(count)
        ]
        for k, (src, dst) in enumerate(arrays)
    ]
    scalars[0].wait()
    for per_array in copies:
        for item in range(count):
            for block in range(blocks):

                @pl.when(start + block * BLOCK < lengths[item])
                def _(copy=per_array[item][block]):
                    copy.start()

    for copy in scalars[1:] + factors:
        copy.wait()
    seed_value = seed[0]
    first = lax.axis_index("dp") * count
    kept = [seed_value * SEED_MUL]
    kept += [offsets[k] for k in range(3)]
    kept += [owners[first + item] for item in range(count)]
    for k, scalar in enumerate(kept):
        scalar_ref[k : k + 1, :] = jnp.full((1, scalar_ref.shape[1]), scalar, jnp.int32)

    def folded(factor, k, first):
        table = rank_rows(seed_value, offsets[3 + k], first)
        return jnp.dot(table, factor[...], preferred_element_type=F32)

    from_query = split_rows(folded(query_up, 0, 0))
    from_value = split_rows(folded(value_up, 1, KR))
    from_hidden = split_rows(folded(query_down, 2, 0) + folded(value_down, 3, KR))

    def project(weights, data):
        product = lax.dot_general(
            weights, data, (((1,), (1,)), ((), ())), preferred_element_type=F32
        )
        return join_rows(product)

    def each_block(visit):
        for item in range(count):
            for block in range(blocks):
                live = start + block * BLOCK < lengths[item]
                visit(item, block, pl.ds(block * BLOCK, BLOCK), pl.ds(item * rows + block * BLOCK, BLOCK), live)

    def keep(item, block):
        position = lax.broadcasted_iota(jnp.int32, (2 * KR, BLOCK), 1)
        return position + (start + block * BLOCK) < lengths[item]

    def upper(item, block, here, out, live):
        @pl.when(live)
        def _():
            copies[0][item][block].wait()
            copies[1][item][block].wait()
            rows_ = project(from_query, query_ref[item, here, :])
            rows_ = rows_ + project(from_value, value_ref[item, here, :])
            side_ref[: 2 * KR, out] = jnp.where(keep(item, block), rows_, 0.0)

        @pl.when(jnp.logical_not(live))
        def _():
            side_ref[: 2 * KR, out] = jnp.zeros((2 * KR, BLOCK), F32)
            query_ref[item, here, :] = jnp.zeros((BLOCK, query_ref.shape[2]), BF16)
            value_ref[item, here, :] = jnp.zeros((BLOCK, value_ref.shape[2]), BF16)

    def lower(item, block, here, out, live):
        @pl.when(live)
        def _():
            copies[2][item][block].wait()
            rows_ = project(from_hidden, hidden_ref[item, here, :])
            side_ref[2 * KR :, out] = jnp.where(keep(item, block), rows_, 0.0)

        @pl.when(jnp.logical_not(live))
        def _():
            side_ref[2 * KR :, out] = jnp.zeros((2 * KR, BLOCK), F32)
            hidden_ref[item, here, :] = jnp.zeros((BLOCK, hidden_ref.shape[2]), BF16)

    each_block(upper)
    each_block(lower)


def table_kernel(step_rows, tables, scalar_ref, *outs):
    shard = lax.axis_index("fsdp")
    seed_term = scalar_ref[0:1, 0:1]
    for k, out in zip(tables, outs):
        rows = out.shape[0]
        row = lax.broadcasted_iota(jnp.int32, (step_rows, KP), 0)
        col = lax.broadcasted_iota(jnp.int32, (step_rows, KP), 1)
        counter = scalar_ref[1 + k : 2 + k, 0:1] + (row + shard * rows) * KP + col
        first = counter * COUNT_MUL + seed_term
        stride = wrapped(step_rows * KP * COUNT_MUL)

        def step(i, values, out=out, stride=stride):
            here = pl.ds(pl.multiple_of(i * step_rows, step_rows), step_rows)
            out[here, :] = centred(values).astype(BF16)
            return values + stride

        lax.fori_loop(0, rows // step_rows, step, first, unroll=4)


def feature_kernel(
    side_ref,
    hidden_ref,
    query_ref,
    value_ref,
    wide_in,
    wide_query,
    wide_value,
    scalar_ref,
    out_ref,
):
    count, rows, _ = hidden_ref.shape
    half = 2 * KR

    def gathered(data_ref, first):
        parts = []
        for item in range(count):
            side = side_ref[first : first + half, item * rows : (item + 1) * rows]
            product = jnp.dot(split_rows(side), data_ref[item], preferred_element_type=F32)
            parts.append(join_rows(product))
        return jnp.concatenate(parts, axis=0)

    def widened(gathered_rows, table):
        product = jnp.dot(split_rows(gathered_rows), table[...], preferred_element_type=F32)
        return join_rows(product)

    side_scale = (R / 3.0) ** (-0.5) / 128.0 * LMAX ** (-0.5) / 128.0
    upper = widened(gathered(hidden_ref, 0), wide_in) * (side_scale * (D / 3.0) ** (-0.5))
    query = widened(gathered(query_ref, half), wide_query) * (side_scale * (DQ / 3.0) ** (-0.5))
    value = widened(gathered(value_ref, half), wide_value) * (side_scale * (DV / 3.0) ** (-0.5))
    group = lax.rem(lax.broadcasted_iota(jnp.int32, query.shape, 0), half)
    lower = jnp.where(group < KR, query, value)
    targets = [scalar_ref[4 + item : 5 + item, 0:1] for item in range(count)]
    halves, spots, pieces, slot_rows, width = out_ref.shape
    slots = slot_rows // KR
    chunks = halves * pieces
    per_block = KP // width
    zero = jnp.zeros((KR, KP), F32)
    for spot in range(spots):
        for block in range(4):
            source, at = (upper, lower)[block // 2], (block % 2) * KR
            wanted = []
            for slot in range(slots):
                total = zero
                for item in range(count):
                    rows_ = source[item * half + at : item * half + at + KR]
                    total = total + jnp.where(targets[item] == spot * slots + slot, rows_, 0.0)
                wanted.append(total)
            wanted = jnp.concatenate(wanted, axis=0)
            for part in range(per_block):
                chunk = block * per_block + part
                if chunk < chunks:
                    out_ref[chunk % halves, spot, chunk // halves] = wanted[
                        :, part * width : (part + 1) * width
                    ]


def finish_kernel(pieces_ref, out_ref):
    sources, _, width = pieces_ref.shape
    total = pieces_ref[0]
    for source in range(1, sources):
        total = total + pieces_ref[source]
    high = total.astype(BF16).astype(F32)
    rest = total - high
    middle = rest.astype(BF16).astype(F32)
    parts = jnp.concatenate([high, middle, rest - middle], axis=0).astype(BF16)
    row = lax.broadcasted_iota(jnp.int32, (width, width * KR), 0)
    col = lax.broadcasted_iota(jnp.int32, (width, width * KR), 1)
    spread = jnp.where(lax.shift_right_logical(col, 2) == row, 1.0, 0.0).astype(BF16)
    wide = jnp.dot(parts, spread, preferred_element_type=F32)
    count = total.shape[0]
    wide = wide[:count] + wide[count : 2 * count] + wide[2 * count :]
    rank = lax.broadcasted_iota(jnp.int32, wide.shape, 0) & (KR - 1)
    place = lax.broadcasted_iota(jnp.int32, wide.shape, 1) & (KR - 1)
    wide = jnp.where(rank == place, wide, 0.0)
    for slot in range(out_ref.shape[0]):
        out_ref[slot : slot + 1, :] = jnp.sum(
            wide[slot * KR : (slot + 1) * KR], axis=0, keepdims=True
        )


def in_vmem():
    return pl.BlockSpec(memory_space=pltpu.VMEM)


def in_hbm():
    return pl.BlockSpec(memory_space=pltpu.HBM)


def per_device(
    hidden_in,
    query_grad,
    value_grad,
    query_down,
    query_up,
    value_down,
    value_up,
    lengths,
    owners,
    proj_seed,
    offsets,
):
    count, rows, in_cols = hidden_in.shape
    q_cols = query_grad.shape[2]
    v_cols = value_grad.shape[2]
    shards = lax.axis_size("fsdp")
    spots = lax.axis_size("dp")
    halves = lax.axis_size("rep")
    side, scalars, hidden, query, value = pl.pallas_call(
        side_kernel,
        out_shape=(
            pltpu.VMEM((4 * KR, count * rows), F32),
            pltpu.VMEM((8, 128), jnp.int32),
            pltpu.VMEM(hidden_in.shape, BF16),
            pltpu.VMEM(query_grad.shape, BF16),
            pltpu.VMEM(value_grad.shape, BF16),
        ),
        in_specs=[in_hbm()] * 11,
        out_specs=[in_vmem()] * 5,
        scratch_shapes=[
            pltpu.VMEM(query_down.shape[::-1], BF16),
            pltpu.VMEM(query_up.shape, BF16),
            pltpu.VMEM(value_down.shape[::-1], BF16),
            pltpu.VMEM(value_up.shape, BF16),
            pltpu.SMEM(lengths.shape, jnp.int32),
            pltpu.SMEM(proj_seed.shape, jnp.int32),
            pltpu.SMEM(offsets.shape, jnp.int32),
            pltpu.SMEM(owners.shape, jnp.int32),
            pltpu.SemaphoreType.DMA((3, count, rows // BLOCK)),
            pltpu.SemaphoreType.DMA((4,)),
            pltpu.SemaphoreType.DMA((4,)),
        ],
        compiler_params=pltpu.CompilerParams(vmem_limit_bytes=42 * 2**20),
        name="sides",
    )(
        hidden_in,
        query_grad,
        value_grad,
        query_down.T,
        query_up,
        value_down.T,
        value_up,
        lengths,
        proj_seed,
        offsets,
        owners,
    )

    def make_tables(which, sizes):
        return pl.pallas_call(
            functools.partial(table_kernel, 32, which),
            out_shape=[pltpu.VMEM((size, KP), BF16) for size in sizes],
            in_specs=[in_vmem()],
            out_specs=[in_vmem()] * len(sizes),
            compiler_params=pltpu.CompilerParams(vmem_limit_bytes=16 * 2**20),
            name="tables",
        )(scalars)

    (wide_in,) = make_tables((0,), (in_cols,))
    hop = 1
    while hop < shards:
        pairs = [(i, i ^ hop) for i in range(shards)]
        side = side + lax.ppermute(side, "fsdp", pairs)
        if hop == 1:
            side, wide_in = lax.optimization_barrier((side, wide_in))
        hop *= 2
    wide_query, wide_value = make_tables((1, 2), (q_cols, v_cols))
    examples = owners.shape[0]
    slots = examples // spots
    width = 4 * KP // (shards * halves)
    pieces = pl.pallas_call(
        feature_kernel,
        out_shape=pltpu.VMEM((halves, spots, shards, slots * KR, width), F32),
        in_specs=[in_vmem()] * 8,
        out_specs=in_vmem(),
        compiler_params=pltpu.CompilerParams(vmem_limit_bytes=16 * 2**20),
        name="features",
    )(side, hidden, query, value, wide_in, wide_query, wide_value, scalars)
    half = lax.axis_index("rep")
    kept = lax.dynamic_index_in_dim(pieces, half, 0, keepdims=False)
    sent = lax.dynamic_index_in_dim(pieces, 1 - half, 0, keepdims=False)
    both = kept + lax.ppermute(sent, "rep", [(0, 1), (1, 0)])
    parts = both.reshape(spots * shards, slots * KR, width)
    parts = lax.all_to_all(parts, ("dp", "fsdp"), 0, 0)
    return pl.pallas_call(
        finish_kernel,
        out_shape=jax.ShapeDtypeStruct((slots, width * KR), F32),
        in_specs=[in_vmem()],
        out_specs=in_vmem(),
        compiler_params=pltpu.CompilerParams(vmem_limit_bytes=16 * 2**20),
        name="finish",
    )(parts)


def solution(mesh):
    placed = (
        P(("groups", "dp"), "rep", "fsdp"),
        P(("groups", "dp"), "rep", "fsdp"),
        P(("groups", "dp"), "rep", "fsdp"),
        P("fsdp", None),
        P(None, "fsdp"),
        P("fsdp", None),
        P(None, "fsdp"),
        P(("groups", "dp")),
        P("groups"),
        P(),
        P(),
    )
    return jax.shard_map(
        per_device,
        mesh=mesh,
        in_specs=placed,
        out_specs=P(("groups", "dp"), ("fsdp", "rep")),
        check_vma=False,
    )
```

```python
import functools

import jax
import jax.numpy as jnp
from jax import lax
from jax.experimental import pallas as pl
from jax.experimental.pallas import tpu as pltpu
from jax.sharding import PartitionSpec as P

D = 8192
DQ = 8192
DV = 1024
R = 64
KP = 512
KR = 4
LMAX = 2048
BLOCK = 256
SEED_MUL = 668265263
COUNT_MUL = -1640531535
BF16 = jnp.bfloat16
F32 = jnp.float32


def mix_bits(values):
    values = values ^ lax.shift_right_logical(values, 15)
    values = values * -2048144777
    values = values ^ lax.shift_right_logical(values, 13)
    values = values * -1028477379
    return values ^ lax.shift_right_logical(values, 16)


def wrapped(value):
    return (value + 2**31) % 2**32 - 2**31


def centred(counter_hash):
    return (mix_bits(counter_hash) & 255).astype(F32) - 127.5


def split_rows(values):
    high = values.astype(BF16).astype(F32)
    return jnp.concatenate([high, values - high], axis=0).astype(BF16)


def join_rows(product):
    half = product.shape[0] // 2
    return product[:half] + product[half:]


def rank_rows(seed_value, offset, first):
    row = lax.broadcasted_iota(jnp.int32, (2 * KR, R), 0) - first
    col = lax.broadcasted_iota(jnp.int32, (2 * KR, R), 1)
    counter = offset + col * KR + row
    entry = centred(counter * COUNT_MUL + seed_value * SEED_MUL)
    return jnp.where((row >= 0) & (row < KR), entry, 0.0).astype(BF16)


def side_kernel(
    hidden_hbm,
    query_hbm,
    value_hbm,
    query_down_hbm,
    query_up_hbm,
    value_down_hbm,
    value_up_hbm,
    lengths_hbm,
    seed_hbm,
    offsets_hbm,
    owners_hbm,
    side_ref,
    scalar_ref,
    hidden_ref,
    query_ref,
    value_ref,
    query_down,
    query_up,
    value_down,
    value_up,
    lengths,
    seed,
    offsets,
    owners,
    block_sem,
    factor_sem,
    scalar_sem,
):
    count, rows, _ = hidden_ref.shape
    blocks = rows // BLOCK
    start = lax.axis_index("rep") * rows
    scalars = [
        pltpu.make_async_copy(src, dst, scalar_sem.at[k])
        for k, (src, dst) in enumerate(
            (
                (lengths_hbm, lengths),
                (seed_hbm, seed),
                (offsets_hbm, offsets),
                (owners_hbm, owners),
            )
        )
    ]
    factors = [
        pltpu.make_async_copy(src, dst, factor_sem.at[k])
        for k, (src, dst) in enumerate(
            (
                (query_up_hbm, query_up),
                (value_up_hbm, value_up),
                (query_down_hbm, query_down),
                (value_down_hbm, value_down),
            )
        )
    ]
    for copy in scalars + factors:
        copy.start()
    arrays = ((query_hbm, query_ref), (value_hbm, value_ref), (hidden_hbm, hidden_ref))
    copies = [
        [
            [
                pltpu.make_async_copy(
                    src.at[item, pl.ds(block * BLOCK, BLOCK)],
                    dst.at[item, pl.ds(block * BLOCK, BLOCK)],
                    block_sem.at[k, item, block],
                )
                for block in range(blocks)
            ]
            for item in range(count)
        ]
        for k, (src, dst) in enumerate(arrays)
    ]
    scalars[0].wait()
    for item in range(count):
        for block in range(blocks):

            @pl.when(start + block * BLOCK < lengths[item])
            def _(item=item, block=block):
                for per_array in copies:
                    per_array[item][block].start()

    for copy in scalars[1:] + factors:
        copy.wait()
    seed_value = seed[0]
    first = lax.axis_index("dp") * count
    kept = [seed_value * SEED_MUL]
    kept += [offsets[k] for k in range(3)]
    kept += [owners[first + item] for item in range(count)]
    for k, scalar in enumerate(kept):
        scalar_ref[k : k + 1, :] = jnp.full((1, scalar_ref.shape[1]), scalar, jnp.int32)

    def folded(factor, k, first):
        table = rank_rows(seed_value, offsets[3 + k], first)
        return jnp.dot(table, factor[...], preferred_element_type=F32)

    from_query = split_rows(folded(query_up, 0, 0))
    from_value = split_rows(folded(value_up, 1, KR))
    from_hidden = split_rows(folded(query_down, 2, 0) + folded(value_down, 3, KR))

    def project(weights, data):
        product = lax.dot_general(
            weights, data, (((1,), (1,)), ((), ())), preferred_element_type=F32
        )
        return join_rows(product)

    for item in range(count):
        for block in range(blocks):
            first = start + block * BLOCK
            live = first < lengths[item]
            here = pl.ds(block * BLOCK, BLOCK)
            out = pl.ds(item * rows + block * BLOCK, BLOCK)

            @pl.when(live)
            def _(item=item, block=block, first=first, here=here, out=out):
                for per_array in copies:
                    per_array[item][block].wait()
                upper = project(from_query, query_ref[item, here, :])
                upper = upper + project(from_value, value_ref[item, here, :])
                lower = project(from_hidden, hidden_ref[item, here, :])
                position = first + lax.broadcasted_iota(jnp.int32, (2 * KR, BLOCK), 1)
                keep = position < lengths[item]
                side_ref[: 2 * KR, out] = jnp.where(keep, upper, 0.0)
                side_ref[2 * KR :, out] = jnp.where(keep, lower, 0.0)

            @pl.when(jnp.logical_not(live))
            def _(item=item, here=here, out=out):
                side_ref[:, out] = jnp.zeros((4 * KR, BLOCK), F32)
                for ref in (query_ref, value_ref, hidden_ref):
                    ref[item, here, :] = jnp.zeros((BLOCK, ref.shape[2]), BF16)


def table_kernel(step_rows, tables, scalar_ref, *outs):
    shard = lax.axis_index("fsdp")
    seed_term = scalar_ref[0:1, 0:1]
    for k, out in zip(tables, outs):
        rows = out.shape[0]
        row = lax.broadcasted_iota(jnp.int32, (step_rows, KP), 0)
        col = lax.broadcasted_iota(jnp.int32, (step_rows, KP), 1)
        counter = scalar_ref[1 + k : 2 + k, 0:1] + (row + shard * rows) * KP + col
        first = counter * COUNT_MUL + seed_term
        stride = wrapped(step_rows * KP * COUNT_MUL)

        def step(i, values, out=out, stride=stride):
            here = pl.ds(pl.multiple_of(i * step_rows, step_rows), step_rows)
            out[here, :] = centred(values).astype(BF16)
            return values + stride

        lax.fori_loop(0, rows // step_rows, step, first, unroll=4)


def feature_kernel(
    side_ref,
    hidden_ref,
    query_ref,
    value_ref,
    wide_in,
    wide_query,
    wide_value,
    scalar_ref,
    kept_ref,
    sent_ref,
):
    count, rows, _ = hidden_ref.shape
    half = 2 * KR

    def gathered(data_ref, first):
        parts = []
        for item in range(count):
            side = side_ref[first : first + half, item * rows : (item + 1) * rows]
            product = jnp.dot(split_rows(side), data_ref[item], preferred_element_type=F32)
            parts.append(join_rows(product))
        return jnp.concatenate(parts, axis=0)

    def widened(gathered_rows, table):
        product = jnp.dot(split_rows(gathered_rows), table[...], preferred_element_type=F32)
        return join_rows(product)

    side_scale = (R / 3.0) ** (-0.5) / 128.0 * LMAX ** (-0.5) / 128.0
    upper = widened(gathered(hidden_ref, 0), wide_in) * (side_scale * (D / 3.0) ** (-0.5))
    query = widened(gathered(query_ref, half), wide_query) * (side_scale * (DQ / 3.0) ** (-0.5))
    value = widened(gathered(value_ref, half), wide_value) * (side_scale * (DV / 3.0) ** (-0.5))
    group = lax.rem(lax.broadcasted_iota(jnp.int32, query.shape, 0), half)
    lower = jnp.where(group < KR, query, value)
    targets = [scalar_ref[4 + item : 5 + item, 0:1] for item in range(count)]
    spots, pieces, slot_rows, width = kept_ref.shape
    slots = slot_rows // KR
    first_half = lax.axis_index("rep") == 0
    per_block = KP // width
    zero = jnp.zeros((KR, KP), F32)
    for spot in range(spots):
        for block in range(4):
            source, at = (upper, lower)[block // 2], (block % 2) * KR
            wanted = []
            for slot in range(slots):
                total = zero
                for item in range(count):
                    rows_ = source[item * half + at : item * half + at + KR]
                    total = total + jnp.where(targets[item] == spot * slots + slot, rows_, 0.0)
                wanted.append(total)
            wanted = jnp.concatenate(wanted, axis=0)
            for chunk in range(block * per_block, (block + 1) * per_block, 2):
                at = (chunk % per_block) * width
                even, odd = wanted[:, at : at + width], wanted[:, at + width : at + 2 * width]
                kept_ref[spot, chunk // 2] = jnp.where(first_half, even, odd)
                sent_ref[spot, chunk // 2] = jnp.where(first_half, odd, even)


def finish_kernel(pieces_ref, out_ref):
    sources, _, width = pieces_ref.shape
    total = pieces_ref[0]
    for source in range(1, sources):
        total = total + pieces_ref[source]
    high = total.astype(BF16).astype(F32)
    rest = total - high
    middle = rest.astype(BF16).astype(F32)
    parts = jnp.concatenate([high, middle, rest - middle], axis=0).astype(BF16)
    row = lax.broadcasted_iota(jnp.int32, (width, width * KR), 0)
    col = lax.broadcasted_iota(jnp.int32, (width, width * KR), 1)
    spread = jnp.where(lax.shift_right_logical(col, 2) == row, 1.0, 0.0).astype(BF16)
    wide = jnp.dot(parts, spread, preferred_element_type=F32)
    count = total.shape[0]
    wide = wide[:count] + wide[count : 2 * count] + wide[2 * count :]
    rank = lax.broadcasted_iota(jnp.int32, wide.shape, 0) & (KR - 1)
    place = lax.broadcasted_iota(jnp.int32, wide.shape, 1) & (KR - 1)
    wide = jnp.where(rank == place, wide, 0.0)
    for slot in range(out_ref.shape[0]):
        out_ref[slot : slot + 1, :] = jnp.sum(
            wide[slot * KR : (slot + 1) * KR], axis=0, keepdims=True
        )


def in_vmem():
    return pl.BlockSpec(memory_space=pltpu.VMEM)


def in_hbm():
    return pl.BlockSpec(memory_space=pltpu.HBM)


def per_device(
    hidden_in,
    query_grad,
    value_grad,
    query_down,
    query_up,
    value_down,
    value_up,
    lengths,
    owners,
    proj_seed,
    offsets,
):
    count, rows, in_cols = hidden_in.shape
    q_cols = query_grad.shape[2]
    v_cols = value_grad.shape[2]
    shards = lax.axis_size("fsdp")
    spots = lax.axis_size("dp")
    side, scalars, hidden, query, value = pl.pallas_call(
        side_kernel,
        out_shape=(
            pltpu.VMEM((4 * KR, count * rows), F32),
            pltpu.VMEM((8, 128), jnp.int32),
            pltpu.VMEM(hidden_in.shape, BF16),
            pltpu.VMEM(query_grad.shape, BF16),
            pltpu.VMEM(value_grad.shape, BF16),
        ),
        in_specs=[in_hbm()] * 11,
        out_specs=[in_vmem()] * 5,
        scratch_shapes=[
            pltpu.VMEM(query_down.shape[::-1], BF16),
            pltpu.VMEM(query_up.shape, BF16),
            pltpu.VMEM(value_down.shape[::-1], BF16),
            pltpu.VMEM(value_up.shape, BF16),
            pltpu.SMEM(lengths.shape, jnp.int32),
            pltpu.SMEM(proj_seed.shape, jnp.int32),
            pltpu.SMEM(offsets.shape, jnp.int32),
            pltpu.SMEM(owners.shape, jnp.int32),
            pltpu.SemaphoreType.DMA((3, count, rows // BLOCK)),
            pltpu.SemaphoreType.DMA((4,)),
            pltpu.SemaphoreType.DMA((4,)),
        ],
        compiler_params=pltpu.CompilerParams(vmem_limit_bytes=42 * 2**20),
        name="sides",
    )(
        hidden_in,
        query_grad,
        value_grad,
        query_down.T,
        query_up,
        value_down.T,
        value_up,
        lengths,
        proj_seed,
        offsets,
        owners,
    )

    def make_tables(which, sizes):
        return pl.pallas_call(
            functools.partial(table_kernel, 32, which),
            out_shape=[pltpu.VMEM((size, KP), BF16) for size in sizes],
            in_specs=[in_vmem()],
            out_specs=[in_vmem()] * len(sizes),
            compiler_params=pltpu.CompilerParams(vmem_limit_bytes=16 * 2**20),
            name="tables",
        )(scalars)

    (wide_in,) = make_tables((0,), (in_cols,))
    hop = 1
    while hop < shards:
        pairs = [(i, i ^ hop) for i in range(shards)]
        side = side + lax.ppermute(side, "fsdp", pairs)
        if hop == 1:
            side, wide_in = lax.optimization_barrier((side, wide_in))
        hop *= 2
    wide_query, wide_value = make_tables((1, 2), (q_cols, v_cols))
    examples = owners.shape[0]
    slots = examples // spots
    width = 4 * KP // (2 * shards)
    kept, sent = pl.pallas_call(
        feature_kernel,
        out_shape=[pltpu.VMEM((spots, shards, slots * KR, width), F32)] * 2,
        in_specs=[in_vmem()] * 8,
        out_specs=[in_vmem()] * 2,
        compiler_params=pltpu.CompilerParams(vmem_limit_bytes=16 * 2**20),
        name="features",
    )(side, hidden, query, value, wide_in, wide_query, wide_value, scalars)
    both = kept + lax.ppermute(sent, "rep", [(0, 1), (1, 0)])
    parts = both.reshape(spots * shards, slots * KR, width)
    parts = lax.all_to_all(parts, ("dp", "fsdp"), 0, 0)
    return pl.pallas_call(
        finish_kernel,
        out_shape=jax.ShapeDtypeStruct((slots, width * KR), F32),
        in_specs=[in_vmem()],
        out_specs=in_vmem(),
        compiler_params=pltpu.CompilerParams(vmem_limit_bytes=16 * 2**20),
        name="finish",
    )(parts)


def solution(mesh):
    placed = (
        P(("groups", "dp"), "rep", "fsdp"),
        P(("groups", "dp"), "rep", "fsdp"),
        P(("groups", "dp"), "rep", "fsdp"),
        P("fsdp", None),
        P(None, "fsdp"),
        P("fsdp", None),
        P(None, "fsdp"),
        P(("groups", "dp")),
        P("groups"),
        P(),
        P(),
    )
    return jax.shard_map(
        per_device,
        mesh=mesh,
        in_specs=placed,
        out_specs=P(("groups", "dp"), ("fsdp", "rep")),
        check_vma=False,
    )
```

```python
import functools

import jax
import jax.numpy as jnp
from jax import lax
from jax.experimental import pallas as pl
from jax.experimental.pallas import tpu as pltpu
from jax.sharding import PartitionSpec as P

D = 8192
DQ = 8192
DV = 1024
R = 64
KP = 512
KR = 4
LMAX = 2048
BLOCK = 256
SEED_MUL = 668265263
COUNT_MUL = -1640531535
BF16 = jnp.bfloat16
F32 = jnp.float32


def mix_bits(values):
    values = values ^ lax.shift_right_logical(values, 15)
    values = values * -2048144777
    values = values ^ lax.shift_right_logical(values, 13)
    values = values * -1028477379
    return values ^ lax.shift_right_logical(values, 16)


def wrapped(value):
    return (value + 2**31) % 2**32 - 2**31


def centred(counter_hash):
    return (mix_bits(counter_hash) & 255).astype(F32) - 127.5


def split_rows(values):
    high = values.astype(BF16).astype(F32)
    return jnp.concatenate([high, values - high], axis=0).astype(BF16)


def join_rows(product):
    half = product.shape[0] // 2
    return product[:half] + product[half:]


def rank_rows(seed_value, offset, first):
    row = lax.broadcasted_iota(jnp.int32, (2 * KR, R), 0) - first
    col = lax.broadcasted_iota(jnp.int32, (2 * KR, R), 1)
    counter = offset + col * KR + row
    entry = centred(counter * COUNT_MUL + seed_value * SEED_MUL)
    return jnp.where((row >= 0) & (row < KR), entry, 0.0).astype(BF16)


def side_kernel(
    hidden_hbm,
    query_hbm,
    value_hbm,
    query_down_hbm,
    query_up_hbm,
    value_down_hbm,
    value_up_hbm,
    lengths_hbm,
    seed_hbm,
    offsets_hbm,
    owners_hbm,
    upper_ref,
    lower_ref,
    scalar_ref,
    hidden_ref,
    query_ref,
    value_ref,
    query_down,
    query_up,
    value_down,
    value_up,
    lengths,
    seed,
    offsets,
    owners,
    block_sem,
    factor_sem,
    scalar_sem,
):
    count, rows, _ = hidden_ref.shape
    blocks = rows // BLOCK
    start = lax.axis_index("rep") * rows
    scalars = [
        pltpu.make_async_copy(src, dst, scalar_sem.at[k])
        for k, (src, dst) in enumerate(
            (
                (lengths_hbm, lengths),
                (seed_hbm, seed),
                (offsets_hbm, offsets),
                (owners_hbm, owners),
            )
        )
    ]
    factors = [
        pltpu.make_async_copy(src, dst, factor_sem.at[k])
        for k, (src, dst) in enumerate(
            (
                (query_up_hbm, query_up),
                (value_up_hbm, value_up),
                (query_down_hbm, query_down),
                (value_down_hbm, value_down),
            )
        )
    ]
    for copy in scalars + factors:
        copy.start()
    arrays = ((query_hbm, query_ref), (value_hbm, value_ref), (hidden_hbm, hidden_ref))
    copies = [
        [
            [
                pltpu.make_async_copy(
                    src.at[item, pl.ds(block * BLOCK, BLOCK)],
                    dst.at[item, pl.ds(block * BLOCK, BLOCK)],
                    block_sem.at[k, item, block],
                )
                for block in range(blocks)
            ]
            for item in range(count)
        ]
        for k, (src, dst) in enumerate(arrays)
    ]
    scalars[0].wait()
    for item in range(count):
        for block in range(blocks):

            @pl.when(start + block * BLOCK < lengths[item])
            def _(item=item, block=block):
                for per_array in copies:
                    per_array[item][block].start()

    for copy in scalars[1:] + factors:
        copy.wait()
    seed_value = seed[0]
    first = lax.axis_index("dp") * count
    kept = [seed_value * SEED_MUL]
    kept += [offsets[k] for k in range(3)]
    kept += [owners[first + item] for item in range(count)]
    for k, scalar in enumerate(kept):
        scalar_ref[k : k + 1, :] = jnp.full((1, scalar_ref.shape[1]), scalar, jnp.int32)

    def folded(factor, k, first):
        table = rank_rows(seed_value, offsets[3 + k], first)
        return jnp.dot(table, factor[...], preferred_element_type=F32)

    from_query = split_rows(folded(query_up, 0, 0))
    from_value = split_rows(folded(value_up, 1, KR))
    from_hidden = split_rows(folded(query_down, 2, 0) + folded(value_down, 3, KR))

    def project(weights, data):
        product = lax.dot_general(
            weights, data, (((1,), (1,)), ((), ())), preferred_element_type=F32
        )
        return join_rows(product)

    for item in range(count):
        for block in range(blocks):
            first = start + block * BLOCK
            live = first < lengths[item]
            here = pl.ds(block * BLOCK, BLOCK)
            out = pl.ds(item * rows + block * BLOCK, BLOCK)

            @pl.when(live)
            def _(item=item, block=block, first=first, here=here, out=out):
                for per_array in copies:
                    per_array[item][block].wait()
                upper = project(from_query, query_ref[item, here, :])
                upper = upper + project(from_value, value_ref[item, here, :])
                lower = project(from_hidden, hidden_ref[item, here, :])
                position = first + lax.broadcasted_iota(jnp.int32, (2 * KR, BLOCK), 1)
                keep = position < lengths[item]
                upper_ref[:, out] = jnp.where(keep, upper, 0.0)
                lower_ref[:, out] = jnp.where(keep, lower, 0.0)

            @pl.when(jnp.logical_not(live))
            def _(item=item, here=here, out=out):
                upper_ref[:, out] = jnp.zeros((2 * KR, BLOCK), F32)
                lower_ref[:, out] = jnp.zeros((2 * KR, BLOCK), F32)
                for ref in (query_ref, value_ref, hidden_ref):
                    ref[item, here, :] = jnp.zeros((BLOCK, ref.shape[2]), BF16)


def table_kernel(step_rows, tables, scalar_ref, *outs):
    shard = lax.axis_index("fsdp")
    seed_term = scalar_ref[0:1, 0:1]
    for k, out in zip(tables, outs):
        rows = out.shape[0]
        row = lax.broadcasted_iota(jnp.int32, (step_rows, KP), 0)
        col = lax.broadcasted_iota(jnp.int32, (step_rows, KP), 1)
        counter = scalar_ref[1 + k : 2 + k, 0:1] + (row + shard * rows) * KP + col
        first = counter * COUNT_MUL + seed_term
        stride = wrapped(step_rows * KP * COUNT_MUL)

        def step(i, values, out=out, stride=stride):
            here = pl.ds(pl.multiple_of(i * step_rows, step_rows), step_rows)
            out[here, :] = centred(values).astype(BF16)
            return values + stride

        lax.fori_loop(0, rows // step_rows, step, first, unroll=4)


SIDE_SCALE = (R / 3.0) ** (-0.5) / 128.0 * LMAX ** (-0.5) / 128.0


def widened(side_ref, data_ref, table, scale):
    count, rows, _ = data_ref.shape
    parts = []
    for item in range(count):
        side = side_ref[:, item * rows : (item + 1) * rows]
        product = jnp.dot(split_rows(side), data_ref[item], preferred_element_type=F32)
        parts.append(join_rows(product))
    gathered = jnp.concatenate(parts, axis=0)
    product = jnp.dot(split_rows(gathered), table[...], preferred_element_type=F32)
    return join_rows(product) * (SIDE_SCALE * scale)


def upper_kernel(side_ref, hidden_ref, wide_in, out_ref):
    out_ref[...] = widened(side_ref, hidden_ref, wide_in, (D / 3.0) ** (-0.5))


def feature_kernel(
    upper_ref,
    side_ref,
    query_ref,
    value_ref,
    wide_query,
    wide_value,
    scalar_ref,
    kept_ref,
    sent_ref,
):
    count = query_ref.shape[0]
    half = 2 * KR
    upper = upper_ref[...]
    query = widened(side_ref, query_ref, wide_query, (DQ / 3.0) ** (-0.5))
    value = widened(side_ref, value_ref, wide_value, (DV / 3.0) ** (-0.5))
    group = lax.rem(lax.broadcasted_iota(jnp.int32, query.shape, 0), half)
    lower = jnp.where(group < KR, query, value)
    targets = [scalar_ref[4 + item : 5 + item, 0:1] for item in range(count)]
    spots, pieces, slot_rows, width = kept_ref.shape
    place = lax.axis_index("dp")
    shard = lax.axis_index("fsdp")
    slots = slot_rows // KR
    first_half = lax.axis_index("rep") == 0
    per_block = KP // width
    zero = jnp.zeros((KR, KP), F32)
    for spot in range(spots):
        for block in range(4):
            source, at = (upper, lower)[block // 2], (block % 2) * KR
            wanted = []
            for slot in range(slots):
                total = zero
                for item in range(count):
                    rows_ = source[item * half + at : item * half + at + KR]
                    total = total + jnp.where(targets[item] == spot * slots + slot, rows_, 0.0)
                wanted.append(total)
            wanted = jnp.concatenate(wanted, axis=0)
            for chunk in range(block * per_block, (block + 1) * per_block, 2):
                at = (chunk % per_block) * width
                even, odd = wanted[:, at : at + width], wanted[:, at + width : at + 2 * width]
                kept_ref[spot ^ place, (chunk // 2) ^ shard] = jnp.where(first_half, even, odd)
                sent_ref[spot ^ place, (chunk // 2) ^ shard] = jnp.where(first_half, odd, even)


def finish_kernel(pieces_ref, out_ref):
    sources, _, width = pieces_ref.shape
    total = pieces_ref[0]
    for source in range(1, sources):
        total = total + pieces_ref[source]
    high = total.astype(BF16).astype(F32)
    rest = total - high
    middle = rest.astype(BF16).astype(F32)
    parts = jnp.concatenate([high, middle, rest - middle], axis=0).astype(BF16)
    row = lax.broadcasted_iota(jnp.int32, (width, width * KR), 0)
    col = lax.broadcasted_iota(jnp.int32, (width, width * KR), 1)
    spread = jnp.where(lax.shift_right_logical(col, 2) == row, 1.0, 0.0).astype(BF16)
    wide = jnp.dot(parts, spread, preferred_element_type=F32)
    count = total.shape[0]
    wide = wide[:count] + wide[count : 2 * count] + wide[2 * count :]
    rank = lax.broadcasted_iota(jnp.int32, wide.shape, 0) & (KR - 1)
    place = lax.broadcasted_iota(jnp.int32, wide.shape, 1) & (KR - 1)
    wide = jnp.where(rank == place, wide, 0.0)
    for slot in range(out_ref.shape[0]):
        out_ref[slot : slot + 1, :] = jnp.sum(
            wide[slot * KR : (slot + 1) * KR], axis=0, keepdims=True
        )


def in_vmem():
    return pl.BlockSpec(memory_space=pltpu.VMEM)


def in_hbm():
    return pl.BlockSpec(memory_space=pltpu.HBM)


def per_device(
    hidden_in,
    query_grad,
    value_grad,
    query_down,
    query_up,
    value_down,
    value_up,
    lengths,
    owners,
    proj_seed,
    offsets,
):
    count, rows, in_cols = hidden_in.shape
    q_cols = query_grad.shape[2]
    v_cols = value_grad.shape[2]
    shards = lax.axis_size("fsdp")
    spots = lax.axis_size("dp")
    upper, lower, scalars, hidden, query, value = pl.pallas_call(
        side_kernel,
        out_shape=(
            pltpu.VMEM((2 * KR, count * rows), F32),
            pltpu.VMEM((2 * KR, count * rows), F32),
            pltpu.VMEM((8, 128), jnp.int32),
            pltpu.VMEM(hidden_in.shape, BF16),
            pltpu.VMEM(query_grad.shape, BF16),
            pltpu.VMEM(value_grad.shape, BF16),
        ),
        in_specs=[in_hbm()] * 11,
        out_specs=[in_vmem()] * 6,
        scratch_shapes=[
            pltpu.VMEM(query_down.shape[::-1], BF16),
            pltpu.VMEM(query_up.shape, BF16),
            pltpu.VMEM(value_down.shape[::-1], BF16),
            pltpu.VMEM(value_up.shape, BF16),
            pltpu.SMEM(lengths.shape, jnp.int32),
            pltpu.SMEM(proj_seed.shape, jnp.int32),
            pltpu.SMEM(offsets.shape, jnp.int32),
            pltpu.SMEM(owners.shape, jnp.int32),
            pltpu.SemaphoreType.DMA((3, count, rows // BLOCK)),
            pltpu.SemaphoreType.DMA((4,)),
            pltpu.SemaphoreType.DMA((4,)),
        ],
        compiler_params=pltpu.CompilerParams(vmem_limit_bytes=42 * 2**20),
        name="sides",
    )(
        hidden_in,
        query_grad,
        value_grad,
        query_down.T,
        query_up,
        value_down.T,
        value_up,
        lengths,
        proj_seed,
        offsets,
        owners,
    )

    def make_tables(which, sizes):
        return pl.pallas_call(
            functools.partial(table_kernel, 32, which),
            out_shape=[pltpu.VMEM((size, KP), BF16) for size in sizes],
            in_specs=[in_vmem()],
            out_specs=[in_vmem()] * len(sizes),
            compiler_params=pltpu.CompilerParams(vmem_limit_bytes=16 * 2**20),
            name="tables",
        )(scalars)

    (wide_in,) = make_tables((0,), (in_cols,))
    wide_query, wide_value = make_tables((1, 2), (q_cols, v_cols))

    hop = 1
    while hop < shards:
        pairs = [(i, i ^ hop) for i in range(shards)]
        moved = lax.ppermute(upper, "fsdp", pairs)
        if hop == 1:
            moved, wide_in = lax.optimization_barrier((moved, wide_in))
        upper = upper + moved
        lower = lower + lax.ppermute(lower, "fsdp", pairs)
        hop *= 2
    upper = pl.pallas_call(
        upper_kernel,
        out_shape=pltpu.VMEM((count * 2 * KR, KP), F32),
        in_specs=[in_vmem()] * 3,
        out_specs=in_vmem(),
        compiler_params=pltpu.CompilerParams(vmem_limit_bytes=16 * 2**20),
        name="upper",
    )(upper, hidden, wide_in)
    examples = owners.shape[0]
    slots = examples // spots
    width = 4 * KP // (2 * shards)
    kept, sent = pl.pallas_call(
        feature_kernel,
        out_shape=[pltpu.VMEM((spots, shards, slots * KR, width), F32)] * 2,
        in_specs=[in_vmem()] * 7,
        out_specs=[in_vmem()] * 2,
        compiler_params=pltpu.CompilerParams(vmem_limit_bytes=16 * 2**20),
        name="features",
    )(upper, lower, query, value, wide_query, wide_value, scalars)
    mine = kept[0] + lax.ppermute(sent[0], "rep", [(0, 1), (1, 0)])
    for hop in range(1, spots):
        straight = [(i, i ^ hop) for i in range(spots)]
        crossed = [(2 * i + r, 2 * (i ^ hop) + 1 - r) for i in range(spots) for r in range(2)]
        mine = mine + lax.ppermute(kept[hop], "dp", straight)
        mine = mine + lax.ppermute(sent[hop], ("dp", "rep"), crossed)
    parts = [mine[0]]
    for hop in range(1, shards):
        parts.append(lax.ppermute(mine[hop], "fsdp", [(i, i ^ hop) for i in range(shards)]))
    parts = jnp.stack(parts)
    return pl.pallas_call(
        finish_kernel,
        out_shape=jax.ShapeDtypeStruct((slots, width * KR), F32),
        in_specs=[in_vmem()],
        out_specs=in_vmem(),
        compiler_params=pltpu.CompilerParams(vmem_limit_bytes=16 * 2**20),
        name="finish",
    )(parts)


def solution(mesh):
    placed = (
        P(("groups", "dp"), "rep", "fsdp"),
        P(("groups", "dp"), "rep", "fsdp"),
        P(("groups", "dp"), "rep", "fsdp"),
        P("fsdp", None),
        P(None, "fsdp"),
        P("fsdp", None),
        P(None, "fsdp"),
        P(("groups", "dp")),
        P("groups"),
        P(),
        P(),
    )
    return jax.shard_map(
        per_device,
        mesh=mesh,
        in_specs=placed,
        out_specs=P(("groups", "dp"), ("fsdp", "rep")),
        check_vma=False,
    )
```

```python
import functools
import math

import jax
import jax.numpy as jnp
from jax import lax
from jax.experimental import pallas as pl
from jax.experimental.pallas import tpu as pltpu
from jax.sharding import PartitionSpec as P

D = 8192
DQ = 8192
DV = 1024
R = 64
KP = 512
KR = 4
LMAX = 2048
BLOCK = 256
SEED_MUL = 668265263
COUNT_MUL = -1640531535
BF16 = jnp.bfloat16
F32 = jnp.float32


def mix_bits(values):
    values = values ^ lax.shift_right_logical(values, 15)
    values = values * -2048144777
    values = values ^ lax.shift_right_logical(values, 13)
    values = values * -1028477379
    return values ^ lax.shift_right_logical(values, 16)


def wrapped(value):
    return (value + 2**31) % 2**32 - 2**31


def centred(counter_hash):
    return (mix_bits(counter_hash) & 255).astype(F32) - 127.5


def split_rows(values):
    high = values.astype(BF16).astype(F32)
    return jnp.concatenate([high, values - high], axis=0).astype(BF16)


def join_rows(product):
    half = product.shape[0] // 2
    return product[:half] + product[half:]


def rank_rows(seed_value, offset, first):
    row = lax.broadcasted_iota(jnp.int32, (2 * KR, R), 0) - first
    col = lax.broadcasted_iota(jnp.int32, (2 * KR, R), 1)
    counter = offset + col * KR + row
    entry = centred(counter * COUNT_MUL + seed_value * SEED_MUL)
    return jnp.where((row >= 0) & (row < KR), entry, 0.0).astype(BF16)


def side_kernel(
    hidden_hbm,
    query_hbm,
    value_hbm,
    query_down_hbm,
    query_up_hbm,
    value_down_hbm,
    value_up_hbm,
    lengths_hbm,
    seed_hbm,
    offsets_hbm,
    owners_hbm,
    upper_ref,
    lower_ref,
    scalar_ref,
    hidden_ref,
    query_ref,
    value_ref,
    query_down,
    query_up,
    value_down,
    value_up,
    lengths,
    seed,
    offsets,
    owners,
    block_sem,
    factor_sem,
    scalar_sem,
):
    count, rows, _ = hidden_ref.shape
    blocks = rows // BLOCK
    start = lax.axis_index("rep") * rows

    def sem_of(ref):
        return 0 if ref.shape[-1] % 128 == 0 else 1

    scalars = [
        pltpu.make_async_copy(src, dst, scalar_sem.at[k])
        for k, (src, dst) in enumerate(
            (
                (lengths_hbm, lengths),
                (seed_hbm, seed),
                (offsets_hbm, offsets),
                (owners_hbm, owners),
            )
        )
    ]
    factors = [
        pltpu.make_async_copy(src, dst, factor_sem.at[sem_of(dst)])
        for src, dst in (
            (query_up_hbm, query_up),
            (value_up_hbm, value_up),
            (query_down_hbm, query_down),
            (value_down_hbm, value_down),
        )
    ]
    for copy in scalars + factors:
        copy.start()
    arrays = ((query_hbm, query_ref), (value_hbm, value_ref), (hidden_hbm, hidden_ref))
    copies = [
        [
            [
                pltpu.make_async_copy(
                    src.at[item, pl.ds(block * BLOCK, BLOCK)],
                    dst.at[item, pl.ds(block * BLOCK, BLOCK)],
                    block_sem.at[sem_of(dst), item, block],
                )
                for block in range(blocks)
            ]
            for item in range(count)
        ]
        for src, dst in arrays
    ]

    def wait_all(pending, dsts, sem):
        amount = sum(math.prod(dst.shape) for dst in dsts if sem_of(dst) == 0)
        part = hidden_ref.at[0, pl.ds(0, amount // hidden_ref.shape[2])]
        pltpu.make_async_copy(part, part, sem).wait()
        for copy, dst in zip(pending, dsts):
            if sem_of(dst):
                copy.wait()

    def block_views(item, block):
        return [dst.at[item, pl.ds(block * BLOCK, BLOCK)] for _, dst in arrays]

    scalars[0].wait()
    def fetch(item):
        for block in range(blocks):

            @pl.when(start + block * BLOCK < lengths[item])
            def _(block=block):
                for per_array in copies:
                    per_array[item][block].start()

    fetch(0)
    wait_all(factors, (query_up, value_up, query_down, value_down), factor_sem.at[0])
    for copy in scalars[1:]:
        copy.wait()
    seed_value = seed[0]
    first = lax.axis_index("dp") * count
    kept = [seed_value * SEED_MUL]
    kept += [offsets[k] for k in range(3)]
    kept += [owners[first + item] for item in range(count)]
    for k, scalar in enumerate(kept):
        scalar_ref[k : k + 1, :] = jnp.full((1, scalar_ref.shape[1]), scalar, jnp.int32)

    def folded(factor, k, first):
        table = rank_rows(seed_value, offsets[3 + k], first)
        return jnp.dot(table, factor[...], preferred_element_type=F32)

    from_query = split_rows(folded(query_up, 0, 0))
    from_value = split_rows(folded(value_up, 1, KR))
    from_hidden = split_rows(folded(query_down, 2, 0) + folded(value_down, 3, KR))

    for item in range(1, count):
        fetch(item)

    def project(weights, ref, item, here):
        width = weights.shape[1]
        step = min(512, width)
        products = [
            lax.dot_general(
                weights[:, at : at + step],
                ref[item, here, at : at + step],
                (((1,), (1,)), ((), ())),
                preferred_element_type=F32,
            )
            for at in range(0, width, step)
        ]
        while len(products) > 1:
            products = [sum(products[k + 1 : k + 2], products[k]) for k in range(0, len(products), 2)]
        return join_rows(products[0])

    for item in range(count):
        for block in range(blocks):
            first = start + block * BLOCK
            live = first < lengths[item]
            here = pl.ds(block * BLOCK, BLOCK)
            out = pl.ds(item * rows + block * BLOCK, BLOCK)

            @pl.when(live)
            def _(item=item, block=block, first=first, here=here, out=out):
                wait_all(
                    [per_array[item][block] for per_array in copies],
                    block_views(item, block),
                    block_sem.at[0, item, block],
                )
                upper = project(from_query, query_ref, item, here)
                upper = upper + project(from_value, value_ref, item, here)
                lower = project(from_hidden, hidden_ref, item, here)
                position = first + lax.broadcasted_iota(jnp.int32, (2 * KR, BLOCK), 1)
                keep = position < lengths[item]
                upper_ref[:, out] = jnp.where(keep, upper, 0.0)
                lower_ref[:, out] = jnp.where(keep, lower, 0.0)

            @pl.when(jnp.logical_not(live))
            def _(item=item, here=here, out=out):
                upper_ref[:, out] = jnp.zeros((2 * KR, BLOCK), F32)
                lower_ref[:, out] = jnp.zeros((2 * KR, BLOCK), F32)
                for ref in (query_ref, value_ref, hidden_ref):
                    ref[item, here, :] = jnp.zeros((BLOCK, ref.shape[2]), BF16)


def table_kernel(step_rows, tables, scalar_ref, *outs):
    shard = lax.axis_index("fsdp")
    seed_term = scalar_ref[0:1, 0:1]
    for k, out in zip(tables, outs):
        rows = out.shape[0]
        row = lax.broadcasted_iota(jnp.int32, (step_rows, KP), 0)
        col = lax.broadcasted_iota(jnp.int32, (step_rows, KP), 1)
        counter = scalar_ref[1 + k : 2 + k, 0:1] + (row + shard * rows) * KP + col
        first = counter * COUNT_MUL + seed_term
        stride = wrapped(step_rows * KP * COUNT_MUL)

        def step(i, values, out=out, stride=stride):
            here = pl.ds(pl.multiple_of(i * step_rows, step_rows), step_rows)
            out[here, :] = centred(values).astype(BF16)
            return values + stride

        lax.fori_loop(0, rows // step_rows, step, first, unroll=4)


SIDE_SCALE = (R / 3.0) ** (-0.5) / 128.0 * LMAX ** (-0.5) / 128.0


def widened(side_ref, data_ref, table, scale):
    count, rows, _ = data_ref.shape
    parts = []
    for item in range(count):
        side = side_ref[:, item * rows : (item + 1) * rows]
        product = jnp.dot(split_rows(side), data_ref[item], preferred_element_type=F32)
        parts.append(join_rows(product))
    gathered = jnp.concatenate(parts, axis=0)
    product = jnp.dot(split_rows(gathered), table[...], preferred_element_type=F32)
    return join_rows(product) * (SIDE_SCALE * scale)


def upper_kernel(side_ref, hidden_ref, wide_in, out_ref):
    out_ref[...] = widened(side_ref, hidden_ref, wide_in, (D / 3.0) ** (-0.5))


def feature_kernel(
    upper_ref,
    side_ref,
    query_ref,
    value_ref,
    wide_query,
    wide_value,
    scalar_ref,
    kept_ref,
    sent_ref,
):
    count = query_ref.shape[0]
    half = 2 * KR
    upper = upper_ref[...]
    query = widened(side_ref, query_ref, wide_query, (DQ / 3.0) ** (-0.5))
    value = widened(side_ref, value_ref, wide_value, (DV / 3.0) ** (-0.5))
    group = lax.rem(lax.broadcasted_iota(jnp.int32, query.shape, 0), half)
    lower = jnp.where(group < KR, query, value)
    targets = [scalar_ref[4 + item : 5 + item, 0:1] for item in range(count)]
    spots, pieces, slot_rows, width = kept_ref.shape
    place = lax.axis_index("dp")
    shard = lax.axis_index("fsdp")
    slots = slot_rows // KR
    first_half = lax.axis_index("rep") == 0
    per_block = KP // width
    zero = jnp.zeros((KR, KP), F32)
    for spot in range(spots):
        for block in range(4):
            source, at = (upper, lower)[block // 2], (block % 2) * KR
            wanted = []
            for slot in range(slots):
                total = zero
                for item in range(count):
                    rows_ = source[item * half + at : item * half + at + KR]
                    total = total + jnp.where(targets[item] == spot * slots + slot, rows_, 0.0)
                wanted.append(total)
            wanted = jnp.concatenate(wanted, axis=0)
            for chunk in range(block * per_block, (block + 1) * per_block, 2):
                at = (chunk % per_block) * width
                even, odd = wanted[:, at : at + width], wanted[:, at + width : at + 2 * width]
                kept_ref[spot ^ place, (chunk // 2) ^ shard] = jnp.where(first_half, even, odd)
                sent_ref[spot ^ place, (chunk // 2) ^ shard] = jnp.where(first_half, odd, even)


def finish_kernel(pieces_ref, out_ref):
    sources, _, width = pieces_ref.shape
    total = pieces_ref[0]
    for source in range(1, sources):
        total = total + pieces_ref[source]
    high = total.astype(BF16).astype(F32)
    rest = total - high
    middle = rest.astype(BF16).astype(F32)
    parts = jnp.concatenate([high, middle, rest - middle], axis=0).astype(BF16)
    row = lax.broadcasted_iota(jnp.int32, (width, width * KR), 0)
    col = lax.broadcasted_iota(jnp.int32, (width, width * KR), 1)
    spread = jnp.where(lax.shift_right_logical(col, 2) == row, 1.0, 0.0).astype(BF16)
    wide = jnp.dot(parts, spread, preferred_element_type=F32)
    count = total.shape[0]
    wide = wide[:count] + wide[count : 2 * count] + wide[2 * count :]
    rank = lax.broadcasted_iota(jnp.int32, wide.shape, 0) & (KR - 1)
    place = lax.broadcasted_iota(jnp.int32, wide.shape, 1) & (KR - 1)
    wide = jnp.where(rank == place, wide, 0.0)
    for slot in range(out_ref.shape[0]):
        out_ref[slot : slot + 1, :] = jnp.sum(
            wide[slot * KR : (slot + 1) * KR], axis=0, keepdims=True
        )


def in_vmem():
    return pl.BlockSpec(memory_space=pltpu.VMEM)


def in_hbm():
    return pl.BlockSpec(memory_space=pltpu.HBM)


def per_device(
    hidden_in,
    query_grad,
    value_grad,
    query_down,
    query_up,
    value_down,
    value_up,
    lengths,
    owners,
    proj_seed,
    offsets,
):
    count, rows, in_cols = hidden_in.shape
    q_cols = query_grad.shape[2]
    v_cols = value_grad.shape[2]
    shards = lax.axis_size("fsdp")
    spots = lax.axis_size("dp")
    upper, lower, scalars, hidden, query, value = pl.pallas_call(
        side_kernel,
        out_shape=(
            pltpu.VMEM((2 * KR, count * rows), F32),
            pltpu.VMEM((2 * KR, count * rows), F32),
            pltpu.VMEM((8, 128), jnp.int32),
            pltpu.VMEM(hidden_in.shape, BF16),
            pltpu.VMEM(query_grad.shape, BF16),
            pltpu.VMEM(value_grad.shape, BF16),
        ),
        in_specs=[in_hbm()] * 11,
        out_specs=[in_vmem()] * 6,
        scratch_shapes=[
            pltpu.VMEM(query_down.shape[::-1], BF16),
            pltpu.VMEM(query_up.shape, BF16),
            pltpu.VMEM(value_down.shape[::-1], BF16),
            pltpu.VMEM(value_up.shape, BF16),
            pltpu.SMEM(lengths.shape, jnp.int32),
            pltpu.SMEM(proj_seed.shape, jnp.int32),
            pltpu.SMEM(offsets.shape, jnp.int32),
            pltpu.SMEM(owners.shape, jnp.int32),
            pltpu.SemaphoreType.DMA((2, count, rows // BLOCK)),
            pltpu.SemaphoreType.DMA((2,)),
            pltpu.SemaphoreType.DMA((4,)),
        ],
        compiler_params=pltpu.CompilerParams(vmem_limit_bytes=42 * 2**20),
        name="sides",
    )(
        hidden_in,
        query_grad,
        value_grad,
        query_down.T,
        query_up,
        value_down.T,
        value_up,
        lengths,
        proj_seed,
        offsets,
        owners,
    )

    def make_tables(which, sizes):
        return pl.pallas_call(
            functools.partial(table_kernel, 32, which),
            out_shape=[pltpu.VMEM((size, KP), BF16) for size in sizes],
            in_specs=[in_vmem()],
            out_specs=[in_vmem()] * len(sizes),
            compiler_params=pltpu.CompilerParams(vmem_limit_bytes=16 * 2**20),
            name="tables",
        )(scalars)

    (wide_in,) = make_tables((0,), (in_cols,))
    wide_query, wide_value = make_tables((1, 2), (q_cols, v_cols))

    hop = 1
    while hop < shards:
        pairs = [(i, i ^ hop) for i in range(shards)]
        moved = lax.ppermute(upper, "fsdp", pairs)
        if hop == 1:
            moved, wide_in = lax.optimization_barrier((moved, wide_in))
        upper = upper + moved
        lower = lower + lax.ppermute(lower, "fsdp", pairs)
        hop *= 2
    upper = pl.pallas_call(
        upper_kernel,
        out_shape=pltpu.VMEM((count * 2 * KR, KP), F32),
        in_specs=[in_vmem()] * 3,
        out_specs=in_vmem(),
        compiler_params=pltpu.CompilerParams(vmem_limit_bytes=16 * 2**20),
        name="upper",
    )(upper, hidden, wide_in)
    examples = owners.shape[0]
    slots = examples // spots
    width = 4 * KP // (2 * shards)
    kept, sent = pl.pallas_call(
        feature_kernel,
        out_shape=[pltpu.VMEM((spots, shards, slots * KR, width), F32)] * 2,
        in_specs=[in_vmem()] * 7,
        out_specs=[in_vmem()] * 2,
        compiler_params=pltpu.CompilerParams(vmem_limit_bytes=16 * 2**20),
        name="features",
    )(upper, lower, query, value, wide_query, wide_value, scalars)
    mine = kept[0] + lax.ppermute(sent[0], "rep", [(0, 1), (1, 0)])
    for hop in range(1, spots):
        straight = [(i, i ^ hop) for i in range(spots)]
        crossed = [(2 * i + r, 2 * (i ^ hop) + 1 - r) for i in range(spots) for r in range(2)]
        mine = mine + lax.ppermute(kept[hop], "dp", straight)
        mine = mine + lax.ppermute(sent[hop], ("dp", "rep"), crossed)
    parts = [mine[0]]
    for hop in range(1, shards):
        parts.append(lax.ppermute(mine[hop], "fsdp", [(i, i ^ hop) for i in range(shards)]))
    parts = jnp.stack(parts)
    return pl.pallas_call(
        finish_kernel,
        out_shape=jax.ShapeDtypeStruct((slots, width * KR), F32),
        in_specs=[in_vmem()],
        out_specs=in_vmem(),
        compiler_params=pltpu.CompilerParams(vmem_limit_bytes=16 * 2**20),
        name="finish",
    )(parts)


def solution(mesh):
    placed = (
        P(("groups", "dp"), "rep", "fsdp"),
        P(("groups", "dp"), "rep", "fsdp"),
        P(("groups", "dp"), "rep", "fsdp"),
        P("fsdp", None),
        P(None, "fsdp"),
        P("fsdp", None),
        P(None, "fsdp"),
        P(("groups", "dp")),
        P("groups"),
        P(),
        P(),
    )
    return jax.shard_map(
        per_device,
        mesh=mesh,
        in_specs=placed,
        out_specs=P(("groups", "dp"), ("fsdp", "rep")),
        check_vma=False,
    )
```

```python
import functools
import math

import jax
import jax.numpy as jnp
from jax import lax
from jax.experimental import pallas as pl
from jax.experimental.pallas import tpu as pltpu
from jax.sharding import PartitionSpec as P

D = 8192
DQ = 8192
DV = 1024
R = 64
KP = 512
KR = 4
LMAX = 2048
BLOCK = 256
SEED_MUL = 668265263
COUNT_MUL = -1640531535
BF16 = jnp.bfloat16
F32 = jnp.float32


def mix_bits(values):
    values = values ^ lax.shift_right_logical(values, 15)
    values = values * -2048144777
    values = values ^ lax.shift_right_logical(values, 13)
    values = values * -1028477379
    return values ^ lax.shift_right_logical(values, 16)


def wrapped(value):
    return (value + 2**31) % 2**32 - 2**31


def centred(counter_hash):
    return (mix_bits(counter_hash) & 255).astype(F32) - 127.5


def split_rows(values):
    high = values.astype(BF16).astype(F32)
    return jnp.concatenate([high, values - high], axis=0).astype(BF16)


def join_rows(product):
    half = product.shape[0] // 2
    return product[:half] + product[half:]


def rank_rows(seed_value, offset, first):
    row = lax.broadcasted_iota(jnp.int32, (2 * KR, R), 0) - first
    col = lax.broadcasted_iota(jnp.int32, (2 * KR, R), 1)
    counter = offset + col * KR + row
    entry = centred(counter * COUNT_MUL + seed_value * SEED_MUL)
    return jnp.where((row >= 0) & (row < KR), entry, 0.0).astype(BF16)


def side_kernel(
    hidden_hbm,
    query_hbm,
    value_hbm,
    query_down_hbm,
    query_up_hbm,
    value_down_hbm,
    value_up_hbm,
    lengths_hbm,
    seed_hbm,
    offsets_hbm,
    owners_hbm,
    upper_ref,
    lower_ref,
    scalar_ref,
    hidden_ref,
    query_ref,
    value_ref,
    query_down,
    query_up,
    value_down,
    value_up,
    lengths,
    seed,
    offsets,
    owners,
    block_sem,
    factor_sem,
    scalar_sem,
):
    count, rows, _ = hidden_ref.shape
    blocks = rows // BLOCK
    start = lax.axis_index("rep") * rows

    def sem_of(ref):
        return 0 if ref.shape[-1] % 128 == 0 else 1

    scalars = [
        pltpu.make_async_copy(src, dst, scalar_sem.at[k])
        for k, (src, dst) in enumerate(
            (
                (lengths_hbm, lengths),
                (seed_hbm, seed),
                (offsets_hbm, offsets),
                (owners_hbm, owners),
            )
        )
    ]
    factors = [
        pltpu.make_async_copy(src, dst, factor_sem.at[sem_of(dst)])
        for src, dst in (
            (query_up_hbm, query_up),
            (value_up_hbm, value_up),
            (query_down_hbm, query_down),
            (value_down_hbm, value_down),
        )
    ]
    for copy in scalars + factors:
        copy.start()
    arrays = ((query_hbm, query_ref), (value_hbm, value_ref), (hidden_hbm, hidden_ref))
    copies = [
        [
            [
                pltpu.make_async_copy(
                    src.at[item, pl.ds(block * BLOCK, BLOCK)],
                    dst.at[item, pl.ds(block * BLOCK, BLOCK)],
                    block_sem.at[sem_of(dst), item, block],
                )
                for block in range(blocks)
            ]
            for item in range(count)
        ]
        for src, dst in arrays
    ]

    def wait_all(pending, dsts, sem):
        amount = sum(math.prod(dst.shape) for dst in dsts if sem_of(dst) == 0)
        part = hidden_ref.at[0, pl.ds(0, amount // hidden_ref.shape[2])]
        pltpu.make_async_copy(part, part, sem).wait()
        for copy, dst in zip(pending, dsts):
            if sem_of(dst):
                copy.wait()

    def block_views(item, block):
        return [dst.at[item, pl.ds(block * BLOCK, BLOCK)] for _, dst in arrays]

    for per_array in copies:
        per_array[0][0].start()
    scalars[0].wait()

    def arrive(item, block):
        wait_all(
            [per_array[item][block] for per_array in copies],
            block_views(item, block),
            block_sem.at[0, item, block],
        )

    def fetch(item):
        for block in range(1 if item == 0 else 0, blocks):

            @pl.when(start + block * BLOCK < lengths[item])
            def _(block=block):
                for per_array in copies:
                    per_array[item][block].start()

    fetch(0)
    wait_all(factors, (query_up, value_up, query_down, value_down), factor_sem.at[0])
    for copy in scalars[1:]:
        copy.wait()
    seed_value = seed[0]
    first = lax.axis_index("dp") * count
    kept = [seed_value * SEED_MUL]
    kept += [offsets[k] for k in range(3)]
    kept += [owners[first + item] for item in range(count)]
    for k, scalar in enumerate(kept):
        scalar_ref[k : k + 1, :] = jnp.full((1, scalar_ref.shape[1]), scalar, jnp.int32)

    def folded(factor, k, first):
        table = rank_rows(seed_value, offsets[3 + k], first)
        return jnp.dot(table, factor[...], preferred_element_type=F32)

    from_query = split_rows(folded(query_up, 0, 0))
    from_value = split_rows(folded(value_up, 1, KR))
    from_hidden = split_rows(folded(query_down, 2, 0) + folded(value_down, 3, KR))

    for item in range(1, count):
        fetch(item)

    def project(weights, ref, item, here):
        width = weights.shape[1]
        step = min(512, width)
        products = [
            lax.dot_general(
                weights[:, at : at + step],
                ref[item, here, at : at + step],
                (((1,), (1,)), ((), ())),
                preferred_element_type=F32,
            )
            for at in range(0, width, step)
        ]
        while len(products) > 1:
            products = [sum(products[k + 1 : k + 2], products[k]) for k in range(0, len(products), 2)]
        return join_rows(products[0])

    for item in range(count):
        for block in range(blocks):
            first = start + block * BLOCK
            live = first < lengths[item]
            here = pl.ds(block * BLOCK, BLOCK)
            out = pl.ds(item * rows + block * BLOCK, BLOCK)

            if not (item or block):
                arrive(item, block)

            @pl.when(live)
            def _(item=item, block=block, first=first, here=here, out=out):
                if item or block:
                    arrive(item, block)
                upper = project(from_query, query_ref, item, here)
                upper = upper + project(from_value, value_ref, item, here)
                lower = project(from_hidden, hidden_ref, item, here)
                position = first + lax.broadcasted_iota(jnp.int32, (2 * KR, BLOCK), 1)
                keep = position < lengths[item]
                upper_ref[:, out] = jnp.where(keep, upper, 0.0)
                lower_ref[:, out] = jnp.where(keep, lower, 0.0)

            @pl.when(jnp.logical_not(live))
            def _(item=item, here=here, out=out):
                upper_ref[:, out] = jnp.zeros((2 * KR, BLOCK), F32)
                lower_ref[:, out] = jnp.zeros((2 * KR, BLOCK), F32)
                for ref in (query_ref, value_ref, hidden_ref):
                    ref[item, here, :] = jnp.zeros((BLOCK, ref.shape[2]), BF16)


def table_kernel(step_rows, tables, scalar_ref, *outs):
    shard = lax.axis_index("fsdp")
    seed_term = scalar_ref[0:1, 0:1]
    for k, out in zip(tables, outs):
        rows = out.shape[0]
        row = lax.broadcasted_iota(jnp.int32, (step_rows, KP), 0)
        col = lax.broadcasted_iota(jnp.int32, (step_rows, KP), 1)
        counter = scalar_ref[1 + k : 2 + k, 0:1] + (row + shard * rows) * KP + col
        first = counter * COUNT_MUL + seed_term
        stride = wrapped(step_rows * KP * COUNT_MUL)

        def step(i, values, out=out, stride=stride):
            here = pl.ds(pl.multiple_of(i * step_rows, step_rows), step_rows)
            out[here, :] = centred(values).astype(BF16)
            return values + stride

        lax.fori_loop(0, rows // step_rows, step, first, unroll=4)


SIDE_SCALE = (R / 3.0) ** (-0.5) / 128.0 * LMAX ** (-0.5) / 128.0


def widened(side_ref, data_ref, table, scale):
    count, rows, _ = data_ref.shape
    parts = []
    for item in range(count):
        side = side_ref[:, item * rows : (item + 1) * rows]
        product = jnp.dot(split_rows(side), data_ref[item], preferred_element_type=F32)
        parts.append(join_rows(product))
    gathered = jnp.concatenate(parts, axis=0)
    product = jnp.dot(split_rows(gathered), table[...], preferred_element_type=F32)
    return join_rows(product) * (SIDE_SCALE * scale)


def upper_kernel(side_ref, hidden_ref, wide_in, out_ref):
    out_ref[...] = widened(side_ref, hidden_ref, wide_in, (D / 3.0) ** (-0.5))


def feature_kernel(
    upper_ref,
    side_ref,
    query_ref,
    value_ref,
    wide_query,
    wide_value,
    scalar_ref,
    kept_ref,
    sent_ref,
):
    count = query_ref.shape[0]
    half = 2 * KR
    upper = upper_ref[...]
    query = widened(side_ref, query_ref, wide_query, (DQ / 3.0) ** (-0.5))
    value = widened(side_ref, value_ref, wide_value, (DV / 3.0) ** (-0.5))
    group = lax.rem(lax.broadcasted_iota(jnp.int32, query.shape, 0), half)
    lower = jnp.where(group < KR, query, value)
    targets = [scalar_ref[4 + item : 5 + item, 0:1] for item in range(count)]
    spots, pieces, slot_rows, width = kept_ref.shape
    place = lax.axis_index("dp")
    shard = lax.axis_index("fsdp")
    slots = slot_rows // KR
    first_half = lax.axis_index("rep") == 0
    per_block = KP // width
    zero = jnp.zeros((KR, KP), F32)
    for spot in range(spots):
        for block in range(4):
            source, at = (upper, lower)[block // 2], (block % 2) * KR
            wanted = []
            for slot in range(slots):
                total = zero
                for item in range(count):
                    rows_ = source[item * half + at : item * half + at + KR]
                    total = total + jnp.where(targets[item] == spot * slots + slot, rows_, 0.0)
                wanted.append(total)
            wanted = jnp.concatenate(wanted, axis=0)
            for chunk in range(block * per_block, (block + 1) * per_block, 2):
                at = (chunk % per_block) * width
                even, odd = wanted[:, at : at + width], wanted[:, at + width : at + 2 * width]
                kept_ref[spot ^ place, lax.rem(chunk // 2 + pieces - shard, pieces)] = jnp.where(first_half, even, odd)
                sent_ref[spot ^ place, lax.rem(chunk // 2 + pieces - shard, pieces)] = jnp.where(first_half, odd, even)


def finish_kernel(pieces_ref, out_ref):
    sources, _, width = pieces_ref.shape
    total = pieces_ref[0]
    for source in range(1, sources):
        total = total + pieces_ref[source]
    high = total.astype(BF16).astype(F32)
    rest = total - high
    middle = rest.astype(BF16).astype(F32)
    parts = jnp.concatenate([high, middle, rest - middle], axis=0).astype(BF16)
    row = lax.broadcasted_iota(jnp.int32, (width, width * KR), 0)
    col = lax.broadcasted_iota(jnp.int32, (width, width * KR), 1)
    spread = jnp.where(lax.shift_right_logical(col, 2) == row, 1.0, 0.0).astype(BF16)
    wide = jnp.dot(parts, spread, preferred_element_type=F32)
    count = total.shape[0]
    wide = wide[:count] + wide[count : 2 * count] + wide[2 * count :]
    rank = lax.broadcasted_iota(jnp.int32, wide.shape, 0) & (KR - 1)
    place = lax.broadcasted_iota(jnp.int32, wide.shape, 1) & (KR - 1)
    wide = jnp.where(rank == place, wide, 0.0)
    for slot in range(out_ref.shape[0]):
        out_ref[slot : slot + 1, :] = jnp.sum(
            wide[slot * KR : (slot + 1) * KR], axis=0, keepdims=True
        )


def in_vmem():
    return pl.BlockSpec(memory_space=pltpu.VMEM)


def in_hbm():
    return pl.BlockSpec(memory_space=pltpu.HBM)


def per_device(
    hidden_in,
    query_grad,
    value_grad,
    query_down,
    query_up,
    value_down,
    value_up,
    lengths,
    owners,
    proj_seed,
    offsets,
):
    count, rows, in_cols = hidden_in.shape
    q_cols = query_grad.shape[2]
    v_cols = value_grad.shape[2]
    shards = lax.axis_size("fsdp")
    spots = lax.axis_size("dp")
    upper, lower, scalars, hidden, query, value = pl.pallas_call(
        side_kernel,
        out_shape=(
            pltpu.VMEM((2 * KR, count * rows), F32),
            pltpu.VMEM((2 * KR, count * rows), F32),
            pltpu.VMEM((8, 128), jnp.int32),
            pltpu.VMEM(hidden_in.shape, BF16),
            pltpu.VMEM(query_grad.shape, BF16),
            pltpu.VMEM(value_grad.shape, BF16),
        ),
        in_specs=[in_hbm()] * 11,
        out_specs=[in_vmem()] * 6,
        scratch_shapes=[
            pltpu.VMEM(query_down.shape[::-1], BF16),
            pltpu.VMEM(query_up.shape, BF16),
            pltpu.VMEM(value_down.shape[::-1], BF16),
            pltpu.VMEM(value_up.shape, BF16),
            pltpu.SMEM(lengths.shape, jnp.int32),
            pltpu.SMEM(proj_seed.shape, jnp.int32),
            pltpu.SMEM(offsets.shape, jnp.int32),
            pltpu.SMEM(owners.shape, jnp.int32),
            pltpu.SemaphoreType.DMA((2, count, rows // BLOCK)),
            pltpu.SemaphoreType.DMA((2,)),
            pltpu.SemaphoreType.DMA((4,)),
        ],
        compiler_params=pltpu.CompilerParams(vmem_limit_bytes=42 * 2**20),
        name="sides",
    )(
        hidden_in,
        query_grad,
        value_grad,
        query_down.T,
        query_up,
        value_down.T,
        value_up,
        lengths,
        proj_seed,
        offsets,
        owners,
    )

    def make_tables(which, sizes):
        return pl.pallas_call(
            functools.partial(table_kernel, 32, which),
            out_shape=[pltpu.VMEM((size, KP), BF16) for size in sizes],
            in_specs=[in_vmem()],
            out_specs=[in_vmem()] * len(sizes),
            compiler_params=pltpu.CompilerParams(vmem_limit_bytes=16 * 2**20),
            name="tables",
        )(scalars)

    (wide_in,) = make_tables((0,), (in_cols,))
    wide_query, wide_value = make_tables((1, 2), (q_cols, v_cols))

    hop = 1
    while hop < shards:
        pairs = [(i, i ^ hop) for i in range(shards)]
        moved = lax.ppermute(upper, "fsdp", pairs)
        if hop == 1:
            moved, wide_in = lax.optimization_barrier((moved, wide_in))
        upper = upper + moved
        lower = lower + lax.ppermute(lower, "fsdp", pairs)
        hop *= 2
    upper = pl.pallas_call(
        upper_kernel,
        out_shape=pltpu.VMEM((count * 2 * KR, KP), F32),
        in_specs=[in_vmem()] * 3,
        out_specs=in_vmem(),
        compiler_params=pltpu.CompilerParams(vmem_limit_bytes=16 * 2**20),
        name="upper",
    )(upper, hidden, wide_in)
    examples = owners.shape[0]
    slots = examples // spots
    width = 4 * KP // (2 * shards)
    kept, sent = pl.pallas_call(
        feature_kernel,
        out_shape=[pltpu.VMEM((spots, shards, slots * KR, width), F32)] * 2,
        in_specs=[in_vmem()] * 7,
        out_specs=[in_vmem()] * 2,
        compiler_params=pltpu.CompilerParams(vmem_limit_bytes=16 * 2**20),
        name="features",
    )(upper, lower, query, value, wide_query, wide_value, scalars)
    moved = []

    def add(value, axis, pairs):
        moved.append(lax.ppermute(value, axis, pairs))

    for hop in range(1, spots):
        add(kept[hop], "dp", [(i, i ^ hop) for i in range(spots)])
    for hop in range(1, spots):
        crossed = [(2 * i + r, 2 * (i ^ hop) + 1 - r) for i in range(spots) for r in range(2)]
        add(sent[hop], ("dp", "rep"), crossed)
    add(sent[0], "rep", [(0, 1), (1, 0)])
    mine = sum(moved, kept[0])
    parts = [mine[0]]
    for hop in range(shards - 1, 0, -1):
        pairs = [(i, (i + hop) % shards) for i in range(shards)]
        parts.append(lax.ppermute(mine[hop], "fsdp", pairs))
    parts = jnp.stack(parts)
    return pl.pallas_call(
        finish_kernel,
        out_shape=jax.ShapeDtypeStruct((slots, width * KR), F32),
        in_specs=[in_vmem()],
        out_specs=in_vmem(),
        compiler_params=pltpu.CompilerParams(vmem_limit_bytes=16 * 2**20),
        name="finish",
    )(parts)


def solution(mesh):
    placed = (
        P(("groups", "dp"), "rep", "fsdp"),
        P(("groups", "dp"), "rep", "fsdp"),
        P(("groups", "dp"), "rep", "fsdp"),
        P("fsdp", None),
        P(None, "fsdp"),
        P("fsdp", None),
        P(None, "fsdp"),
        P(("groups", "dp")),
        P("groups"),
        P(),
        P(),
    )
    return jax.shard_map(
        per_device,
        mesh=mesh,
        in_specs=placed,
        out_specs=P(("groups", "dp"), ("fsdp", "rep")),
        check_vma=False,
    )
```

```python
import functools
import math

import jax
import jax.numpy as jnp
from jax import lax
from jax.experimental import pallas as pl
from jax.experimental.pallas import tpu as pltpu
from jax.sharding import PartitionSpec as P

D = 8192
DQ = 8192
DV = 1024
R = 64
KP = 512
KR = 4
LMAX = 2048
BLOCK = 256
SEED_MUL = 668265263
COUNT_MUL = -1640531535
BF16 = jnp.bfloat16
F32 = jnp.float32


def mix_bits(values):
    values = values ^ lax.shift_right_logical(values, 15)
    values = values * -2048144777
    values = values ^ lax.shift_right_logical(values, 13)
    values = values * -1028477379
    return values ^ lax.shift_right_logical(values, 16)


def wrapped(value):
    return (value + 2**31) % 2**32 - 2**31


def centred(counter_hash):
    return (mix_bits(counter_hash) & 255).astype(F32) - 127.5


def split_rows(values):
    high = values.astype(BF16).astype(F32)
    return jnp.concatenate([high, values - high], axis=0).astype(BF16)


def join_rows(product):
    half = product.shape[0] // 2
    return product[:half] + product[half:]


def rank_rows(seed_value, offset, first):
    row = lax.broadcasted_iota(jnp.int32, (2 * KR, R), 0) - first
    col = lax.broadcasted_iota(jnp.int32, (2 * KR, R), 1)
    counter = offset + col * KR + row
    entry = centred(counter * COUNT_MUL + seed_value * SEED_MUL)
    return jnp.where((row >= 0) & (row < KR), entry, 0.0).astype(BF16)


def side_kernel(
    hidden_hbm,
    query_hbm,
    value_hbm,
    query_down_hbm,
    query_up_hbm,
    value_down_hbm,
    value_up_hbm,
    lengths_hbm,
    seed_hbm,
    offsets_hbm,
    owners_hbm,
    upper_ref,
    lower_ref,
    scalar_ref,
    hidden_ref,
    query_ref,
    value_ref,
    query_down,
    query_up,
    value_down,
    value_up,
    lengths,
    seed,
    offsets,
    owners,
    block_sem,
    factor_sem,
    scalar_sem,
):
    count, rows, _ = hidden_ref.shape
    blocks = rows // BLOCK
    start = lax.axis_index("rep") * rows

    def sem_of(ref):
        return 0 if ref.shape[-1] % 128 == 0 else 1

    scalars = [
        pltpu.make_async_copy(src, dst, scalar_sem.at[k])
        for k, (src, dst) in enumerate(
            (
                (lengths_hbm, lengths),
                (seed_hbm, seed),
                (offsets_hbm, offsets),
                (owners_hbm, owners),
            )
        )
    ]
    factors = [
        pltpu.make_async_copy(src, dst, factor_sem.at[k])
        for src, dst, k in (
            (query_up_hbm, query_up, 0),
            (query_down_hbm, query_down, 0),
            (value_down_hbm, value_down, 0),
            (value_up_hbm, value_up, 1),
        )
    ]
    for copy in scalars + factors:
        copy.start()
    arrays = ((query_hbm, query_ref), (value_hbm, value_ref), (hidden_hbm, hidden_ref))
    copies = [
        [
            [
                pltpu.make_async_copy(
                    src.at[item, pl.ds(block * BLOCK, BLOCK)],
                    dst.at[item, pl.ds(block * BLOCK, BLOCK)],
                    block_sem.at[sem_of(dst), item, block],
                )
                for block in range(blocks)
            ]
            for item in range(count)
        ]
        for src, dst in arrays
    ]

    def wait_all(pending, dsts, sem):
        amount = sum(math.prod(dst.shape) for dst in dsts if sem_of(dst) == 0)
        part = hidden_ref.at[0, pl.ds(0, amount // hidden_ref.shape[2])]
        pltpu.make_async_copy(part, part, sem).wait()
        for copy, dst in zip(pending, dsts):
            if sem_of(dst):
                copy.wait()

    def block_views(item, block):
        return [dst.at[item, pl.ds(block * BLOCK, BLOCK)] for _, dst in arrays]

    for per_array in copies:
        per_array[0][0].start()
    scalars[0].wait()

    def arrive(item, block):
        wait_all(
            [per_array[item][block] for per_array in copies],
            block_views(item, block),
            block_sem.at[0, item, block],
        )

    def fetch(item):
        for block in range(1 if item == 0 else 0, blocks):

            @pl.when(start + block * BLOCK < lengths[item])
            def _(block=block):
                for per_array in copies:
                    per_array[item][block].start()

    fetch(0)
    wait_all(factors[:3], (query_up, query_down, value_down), factor_sem.at[0])
    factors[3].wait()
    for copy in scalars[1:]:
        copy.wait()
    seed_value = seed[0]
    first = lax.axis_index("dp") * count
    kept = [seed_value * SEED_MUL]
    kept += [offsets[k] for k in range(3)]
    kept += [owners[first + item] for item in range(count)]
    for k, scalar in enumerate(kept):
        scalar_ref[k : k + 1, :] = jnp.full((1, scalar_ref.shape[1]), scalar, jnp.int32)

    def folded(factor, k, first):
        table = rank_rows(seed_value, offsets[3 + k], first)
        return jnp.dot(table, factor[...], preferred_element_type=F32)

    from_query = split_rows(folded(query_up, 0, 0))
    from_value = split_rows(folded(value_up, 1, KR))
    from_hidden = split_rows(folded(query_down, 2, 0) + folded(value_down, 3, KR))

    for item in range(1, count):
        fetch(item)

    def project(weights, ref, item, here):
        width = weights.shape[1]
        step = min(512, width)
        products = [
            lax.dot_general(
                weights[:, at : at + step],
                ref[item, here, at : at + step],
                (((1,), (1,)), ((), ())),
                preferred_element_type=F32,
            )
            for at in range(0, width, step)
        ]
        while len(products) > 1:
            products = [sum(products[k + 1 : k + 2], products[k]) for k in range(0, len(products), 2)]
        return join_rows(products[0])

    for item in range(count):
        for block in range(blocks):
            first = start + block * BLOCK
            live = first < lengths[item]
            here = pl.ds(block * BLOCK, BLOCK)
            out = pl.ds(item * rows + block * BLOCK, BLOCK)

            if not (item or block):
                arrive(item, block)

            @pl.when(live)
            def _(item=item, block=block, first=first, here=here, out=out):
                if item or block:
                    arrive(item, block)
                upper = project(from_query, query_ref, item, here)
                upper = upper + project(from_value, value_ref, item, here)
                lower = project(from_hidden, hidden_ref, item, here)
                position = first + lax.broadcasted_iota(jnp.int32, (2 * KR, BLOCK), 1)
                keep = position < lengths[item]
                upper_ref[:, out] = jnp.where(keep, upper, 0.0)
                lower_ref[:, out] = jnp.where(keep, lower, 0.0)

            @pl.when(jnp.logical_not(live))
            def _(item=item, here=here, out=out):
                upper_ref[:, out] = jnp.zeros((2 * KR, BLOCK), F32)
                lower_ref[:, out] = jnp.zeros((2 * KR, BLOCK), F32)
                for ref in (query_ref, value_ref, hidden_ref):
                    ref[item, here, :] = jnp.zeros((BLOCK, ref.shape[2]), BF16)


def table_kernel(step_rows, tables, scalar_ref, *outs):
    shard = lax.axis_index("fsdp")
    seed_term = scalar_ref[0:1, 0:1]
    for k, out in zip(tables, outs):
        rows = out.shape[0]
        row = lax.broadcasted_iota(jnp.int32, (step_rows, KP), 0)
        col = lax.broadcasted_iota(jnp.int32, (step_rows, KP), 1)
        counter = scalar_ref[1 + k : 2 + k, 0:1] + (row + shard * rows) * KP + col
        first = counter * COUNT_MUL + seed_term
        stride = wrapped(step_rows * KP * COUNT_MUL)

        def step(i, values, out=out, stride=stride):
            here = pl.ds(pl.multiple_of(i * step_rows, step_rows), step_rows)
            out[here, :] = centred(values).astype(BF16)
            return values + stride

        lax.fori_loop(0, rows // step_rows, step, first, unroll=4)


SIDE_SCALE = (R / 3.0) ** (-0.5) / 128.0 * LMAX ** (-0.5) / 128.0


def widened(side_ref, data_ref, table, scale):
    count, rows, _ = data_ref.shape
    parts = []
    for item in range(count):
        side = side_ref[:, item * rows : (item + 1) * rows]
        product = jnp.dot(split_rows(side), data_ref[item], preferred_element_type=F32)
        parts.append(join_rows(product))
    gathered = jnp.concatenate(parts, axis=0)
    product = jnp.dot(split_rows(gathered), table[...], preferred_element_type=F32)
    return join_rows(product) * (SIDE_SCALE * scale)


def upper_kernel(side_ref, hidden_ref, wide_in, out_ref):
    out_ref[...] = widened(side_ref, hidden_ref, wide_in, (D / 3.0) ** (-0.5))


def feature_kernel(
    upper_ref,
    side_ref,
    query_ref,
    value_ref,
    wide_query,
    wide_value,
    scalar_ref,
    kept_ref,
    sent_ref,
):
    count = query_ref.shape[0]
    half = 2 * KR
    upper = upper_ref[...]
    query = widened(side_ref, query_ref, wide_query, (DQ / 3.0) ** (-0.5))
    value = widened(side_ref, value_ref, wide_value, (DV / 3.0) ** (-0.5))
    group = lax.rem(lax.broadcasted_iota(jnp.int32, query.shape, 0), half)
    lower = jnp.where(group < KR, query, value)
    targets = [scalar_ref[4 + item : 5 + item, 0:1] for item in range(count)]
    spots, pieces, slot_rows, width = kept_ref.shape
    place = lax.axis_index("dp")
    shard = lax.axis_index("fsdp")
    slots = slot_rows // KR
    first_half = lax.axis_index("rep") == 0
    per_block = KP // width
    zero = jnp.zeros((KR, KP), F32)
    for spot in range(spots):
        for block in range(4):
            source, at = (upper, lower)[block // 2], (block % 2) * KR
            wanted = []
            for slot in range(slots):
                total = zero
                for item in range(count):
                    rows_ = source[item * half + at : item * half + at + KR]
                    total = total + jnp.where(targets[item] == spot * slots + slot, rows_, 0.0)
                wanted.append(total)
            wanted = jnp.concatenate(wanted, axis=0)
            for chunk in range(block * per_block, (block + 1) * per_block, 2):
                at = (chunk % per_block) * width
                even, odd = wanted[:, at : at + width], wanted[:, at + width : at + 2 * width]
                kept_ref[spot ^ place, lax.rem(chunk // 2 + pieces - shard, pieces)] = jnp.where(first_half, even, odd)
                sent_ref[spot ^ place, lax.rem(chunk // 2 + pieces - shard, pieces)] = jnp.where(first_half, odd, even)


def finish_kernel(pieces_ref, out_ref):
    sources, _, width = pieces_ref.shape
    total = pieces_ref[0]
    for source in range(1, sources):
        total = total + pieces_ref[source]
    high = total.astype(BF16).astype(F32)
    rest = total - high
    middle = rest.astype(BF16).astype(F32)
    parts = jnp.concatenate([high, middle, rest - middle], axis=0).astype(BF16)
    row = lax.broadcasted_iota(jnp.int32, (width, width * KR), 0)
    col = lax.broadcasted_iota(jnp.int32, (width, width * KR), 1)
    spread = jnp.where(lax.shift_right_logical(col, 2) == row, 1.0, 0.0).astype(BF16)
    wide = jnp.dot(parts, spread, preferred_element_type=F32)
    count = total.shape[0]
    wide = wide[:count] + wide[count : 2 * count] + wide[2 * count :]
    rank = lax.broadcasted_iota(jnp.int32, wide.shape, 0) & (KR - 1)
    place = lax.broadcasted_iota(jnp.int32, wide.shape, 1) & (KR - 1)
    wide = jnp.where(rank == place, wide, 0.0)
    for slot in range(out_ref.shape[0]):
        out_ref[slot : slot + 1, :] = jnp.sum(
            wide[slot * KR : (slot + 1) * KR], axis=0, keepdims=True
        )


def in_vmem():
    return pl.BlockSpec(memory_space=pltpu.VMEM)


def in_hbm():
    return pl.BlockSpec(memory_space=pltpu.HBM)


def per_device(
    hidden_in,
    query_grad,
    value_grad,
    query_down,
    query_up,
    value_down,
    value_up,
    lengths,
    owners,
    proj_seed,
    offsets,
):
    count, rows, in_cols = hidden_in.shape
    q_cols = query_grad.shape[2]
    v_cols = value_grad.shape[2]
    shards = lax.axis_size("fsdp")
    spots = lax.axis_size("dp")
    upper, lower, scalars, hidden, query, value = pl.pallas_call(
        side_kernel,
        out_shape=(
            pltpu.VMEM((2 * KR, count * rows), F32),
            pltpu.VMEM((2 * KR, count * rows), F32),
            pltpu.VMEM((8, 128), jnp.int32),
            pltpu.VMEM(hidden_in.shape, BF16),
            pltpu.VMEM(query_grad.shape, BF16),
            pltpu.VMEM(value_grad.shape, BF16),
        ),
        in_specs=[in_hbm()] * 11,
        out_specs=[in_vmem()] * 6,
        scratch_shapes=[
            pltpu.VMEM(query_down.shape[::-1], BF16),
            pltpu.VMEM(query_up.shape, BF16),
            pltpu.VMEM(value_down.shape[::-1], BF16),
            pltpu.VMEM(value_up.shape, BF16),
            pltpu.SMEM(lengths.shape, jnp.int32),
            pltpu.SMEM(proj_seed.shape, jnp.int32),
            pltpu.SMEM(offsets.shape, jnp.int32),
            pltpu.SMEM(owners.shape, jnp.int32),
            pltpu.SemaphoreType.DMA((2, count, rows // BLOCK)),
            pltpu.SemaphoreType.DMA((2,)),
            pltpu.SemaphoreType.DMA((4,)),
        ],
        compiler_params=pltpu.CompilerParams(vmem_limit_bytes=42 * 2**20),
        name="sides",
    )(
        hidden_in,
        query_grad,
        value_grad,
        query_down.T,
        query_up,
        value_down.T,
        value_up,
        lengths,
        proj_seed,
        offsets,
        owners,
    )

    def make_tables(which, sizes):
        return pl.pallas_call(
            functools.partial(table_kernel, 32, which),
            out_shape=[pltpu.VMEM((size, KP), BF16) for size in sizes],
            in_specs=[in_vmem()],
            out_specs=[in_vmem()] * len(sizes),
            compiler_params=pltpu.CompilerParams(vmem_limit_bytes=16 * 2**20),
            name="tables",
        )(scalars)

    (wide_in,) = make_tables((0,), (in_cols,))
    wide_query, wide_value = make_tables((1, 2), (q_cols, v_cols))

    hop = 1
    while hop < shards:
        pairs = [(i, i ^ hop) for i in range(shards)]
        moved = lax.ppermute(upper, "fsdp", pairs)
        lower_moved = lax.ppermute(lower, "fsdp", pairs)
        if hop == 1:
            lower_moved, wide_in = lax.optimization_barrier((lower_moved, wide_in))
        upper = upper + moved
        lower = lower + lower_moved
        hop *= 2
    upper = pl.pallas_call(
        upper_kernel,
        out_shape=pltpu.VMEM((count * 2 * KR, KP), F32),
        in_specs=[in_vmem()] * 3,
        out_specs=in_vmem(),
        compiler_params=pltpu.CompilerParams(vmem_limit_bytes=16 * 2**20),
        name="upper",
    )(upper, hidden, wide_in)
    examples = owners.shape[0]
    slots = examples // spots
    width = 4 * KP // (2 * shards)
    kept, sent = pl.pallas_call(
        feature_kernel,
        out_shape=[pltpu.VMEM((spots, shards, slots * KR, width), F32)] * 2,
        in_specs=[in_vmem()] * 7,
        out_specs=[in_vmem()] * 2,
        compiler_params=pltpu.CompilerParams(vmem_limit_bytes=16 * 2**20),
        name="features",
    )(upper, lower, query, value, wide_query, wide_value, scalars)
    moved = []

    def add(value, axis, pairs):
        moved.append(lax.ppermute(value, axis, pairs))

    for hop in range(1, spots):
        add(kept[hop], "dp", [(i, i ^ hop) for i in range(spots)])
    for hop in range(1, spots):
        crossed = [(2 * i + r, 2 * (i ^ hop) + 1 - r) for i in range(spots) for r in range(2)]
        add(sent[hop], ("dp", "rep"), crossed)
    add(sent[0], "rep", [(0, 1), (1, 0)])
    mine = sum(moved, kept[0])
    parts = [mine[0]]
    for hop in range(shards - 1, 0, -1):
        pairs = [(i, (i + hop) % shards) for i in range(shards)]
        parts.append(lax.ppermute(mine[hop], "fsdp", pairs))
    parts = jnp.stack(parts)
    return pl.pallas_call(
        finish_kernel,
        out_shape=jax.ShapeDtypeStruct((slots, width * KR), F32),
        in_specs=[in_vmem()],
        out_specs=in_vmem(),
        compiler_params=pltpu.CompilerParams(vmem_limit_bytes=16 * 2**20),
        name="finish",
    )(parts)


def solution(mesh):
    placed = (
        P(("groups", "dp"), "rep", "fsdp"),
        P(("groups", "dp"), "rep", "fsdp"),
        P(("groups", "dp"), "rep", "fsdp"),
        P("fsdp", None),
        P(None, "fsdp"),
        P("fsdp", None),
        P(None, "fsdp"),
        P(("groups", "dp")),
        P("groups"),
        P(),
        P(),
    )
    return jax.shard_map(
        per_device,
        mesh=mesh,
        in_specs=placed,
        out_specs=P(("groups", "dp"), ("fsdp", "rep")),
        check_vma=False,
    )
```

```python
import functools
import math

import jax
import jax.numpy as jnp
from jax import lax
from jax.experimental import pallas as pl
from jax.experimental.pallas import tpu as pltpu
from jax.sharding import PartitionSpec as P

D = 8192
DQ = 8192
DV = 1024
R = 64
KP = 512
KR = 4
LMAX = 2048
BLOCK = 256
SEED_MUL = 668265263
COUNT_MUL = -1640531535
BF16 = jnp.bfloat16
F32 = jnp.float32


def mix_bits(values):
    values = values ^ lax.shift_right_logical(values, 15)
    values = values * -2048144777
    values = values ^ lax.shift_right_logical(values, 13)
    values = values * -1028477379
    return values ^ lax.shift_right_logical(values, 16)


def wrapped(value):
    return (value + 2**31) % 2**32 - 2**31


def centred(counter_hash):
    return (mix_bits(counter_hash) & 255).astype(F32) - 127.5


def split_rows(values):
    high = values.astype(BF16).astype(F32)
    return jnp.concatenate([high, values - high], axis=0).astype(BF16)


def join_rows(product):
    half = product.shape[0] // 2
    return product[:half] + product[half:]


def rank_rows(seed_value, offset, first):
    row = lax.broadcasted_iota(jnp.int32, (2 * KR, R), 0) - first
    col = lax.broadcasted_iota(jnp.int32, (2 * KR, R), 1)
    counter = offset + col * KR + row
    entry = centred(counter * COUNT_MUL + seed_value * SEED_MUL)
    return jnp.where((row >= 0) & (row < KR), entry, 0.0).astype(BF16)


def side_kernel(
    hidden_hbm,
    query_hbm,
    value_hbm,
    query_down_hbm,
    query_up_hbm,
    value_down_hbm,
    value_up_hbm,
    lengths_hbm,
    seed_hbm,
    offsets_hbm,
    owners_hbm,
    upper_ref,
    lower_ref,
    scalar_ref,
    hidden_ref,
    query_ref,
    value_ref,
    query_down,
    query_up,
    value_down,
    value_up,
    lengths,
    seed,
    offsets,
    owners,
    block_sem,
    factor_sem,
    scalar_sem,
):
    count, rows, _ = hidden_ref.shape
    blocks = rows // BLOCK
    start = lax.axis_index("rep") * rows

    def sem_of(ref):
        return 0 if ref.shape[-1] % 128 == 0 else 1

    scalars = [
        pltpu.make_async_copy(src, dst, scalar_sem.at[k])
        for k, (src, dst) in enumerate(
            (
                (lengths_hbm, lengths),
                (seed_hbm, seed),
                (offsets_hbm, offsets),
                (owners_hbm, owners),
            )
        )
    ]
    factors = [
        pltpu.make_async_copy(src, dst, factor_sem.at[k])
        for src, dst, k in (
            (query_up_hbm, query_up, 0),
            (query_down_hbm, query_down, 0),
            (value_down_hbm, value_down, 0),
            (value_up_hbm, value_up, 1),
        )
    ]
    for copy in scalars + factors:
        copy.start()
    arrays = ((query_hbm, query_ref), (value_hbm, value_ref), (hidden_hbm, hidden_ref))
    copies = [
        [
            [
                pltpu.make_async_copy(
                    src.at[item, pl.ds(block * BLOCK, BLOCK)],
                    dst.at[item, pl.ds(block * BLOCK, BLOCK)],
                    block_sem.at[sem_of(dst), item, block],
                )
                for block in range(blocks)
            ]
            for item in range(count)
        ]
        for src, dst in arrays
    ]

    def wait_all(pending, dsts, sem):
        amount = sum(math.prod(dst.shape) for dst in dsts if sem_of(dst) == 0)
        part = hidden_ref.at[0, pl.ds(0, amount // hidden_ref.shape[2])]
        pltpu.make_async_copy(part, part, sem).wait()
        for copy, dst in zip(pending, dsts):
            if sem_of(dst):
                copy.wait()

    def block_views(item, block):
        return [dst.at[item, pl.ds(block * BLOCK, BLOCK)] for _, dst in arrays]

    for per_array in copies:
        per_array[0][0].start()
    scalars[0].wait()

    def arrive(item, block):
        wait_all(
            [per_array[item][block] for per_array in copies],
            block_views(item, block),
            block_sem.at[0, item, block],
        )

    def fetch(item):
        for block in range(1 if item == 0 else 0, blocks):

            @pl.when(start + block * BLOCK < lengths[item])
            def _(block=block):
                for per_array in copies:
                    per_array[item][block].start()

    fetch(0)
    wait_all(factors[:3], (query_up, query_down, value_down), factor_sem.at[0])
    factors[3].wait()
    for copy in scalars[1:]:
        copy.wait()
    seed_value = seed[0]
    first = lax.axis_index("dp") * count
    kept = [seed_value * SEED_MUL]
    kept += [offsets[k] for k in range(3)]
    kept += [owners[first + item] for item in range(count)]
    for k, scalar in enumerate(kept):
        scalar_ref[k : k + 1, :] = jnp.full((1, scalar_ref.shape[1]), scalar, jnp.int32)

    def folded(factor, k, first):
        table = rank_rows(seed_value, offsets[3 + k], first)
        return jnp.dot(table, factor[...], preferred_element_type=F32)

    from_query = split_rows(folded(query_up, 0, 0))
    from_value = split_rows(folded(value_up, 1, KR))
    from_hidden = split_rows(folded(query_down, 2, 0) + folded(value_down, 3, KR))

    for item in range(1, count):
        fetch(item)

    def project(weights, ref, item, here):
        width = weights.shape[1]
        step = min(512, width)
        products = [
            lax.dot_general(
                weights[:, at : at + step],
                ref[item, here, at : at + step],
                (((1,), (1,)), ((), ())),
                preferred_element_type=F32,
            )
            for at in range(0, width, step)
        ]
        while len(products) > 1:
            products = [sum(products[k + 1 : k + 2], products[k]) for k in range(0, len(products), 2)]
        return join_rows(products[0])

    for item in range(count):
        for block in range(blocks):
            first = start + block * BLOCK
            live = first < lengths[item]
            here = pl.ds(block * BLOCK, BLOCK)
            out = pl.ds(item * rows + block * BLOCK, BLOCK)

            if not (item or block):
                arrive(item, block)

            @pl.when(live)
            def _(item=item, block=block, first=first, here=here, out=out):
                if item or block:
                    arrive(item, block)
                upper = project(from_query, query_ref, item, here)
                upper = upper + project(from_value, value_ref, item, here)
                lower = project(from_hidden, hidden_ref, item, here)
                position = first + lax.broadcasted_iota(jnp.int32, (2 * KR, BLOCK), 1)
                keep = position < lengths[item]
                upper_ref[:, out] = jnp.where(keep, upper, 0.0)
                lower_ref[:, out] = jnp.where(keep, lower, 0.0)

            @pl.when(jnp.logical_not(live))
            def _(item=item, here=here, out=out):
                upper_ref[:, out] = jnp.zeros((2 * KR, BLOCK), F32)
                lower_ref[:, out] = jnp.zeros((2 * KR, BLOCK), F32)
                for ref in (query_ref, value_ref, hidden_ref):
                    ref[item, here, :] = jnp.zeros((BLOCK, ref.shape[2]), BF16)


def table_kernel(step_rows, tables, scalar_ref, *outs):
    shard = lax.axis_index("fsdp")
    seed_term = scalar_ref[0:1, 0:1]
    for k, out in zip(tables, outs):
        rows = out.shape[0]
        row = lax.broadcasted_iota(jnp.int32, (step_rows, KP), 0)
        col = lax.broadcasted_iota(jnp.int32, (step_rows, KP), 1)
        counter = scalar_ref[1 + k : 2 + k, 0:1] + (row + shard * rows) * KP + col
        first = counter * COUNT_MUL + seed_term
        stride = wrapped(step_rows * KP * COUNT_MUL)

        def step(i, values, out=out, stride=stride):
            here = pl.ds(pl.multiple_of(i * step_rows, step_rows), step_rows)
            out[here, :] = centred(values).astype(BF16)
            return values + stride

        lax.fori_loop(0, rows // step_rows, step, first, unroll=4)


SIDE_SCALE = (R / 3.0) ** (-0.5) / 128.0 * LMAX ** (-0.5) / 128.0


def widened(side_ref, data_ref, table, scale):
    count, rows, _ = data_ref.shape
    parts = []
    for item in range(count):
        side = side_ref[:, item * rows : (item + 1) * rows]
        product = jnp.dot(split_rows(side), data_ref[item], preferred_element_type=F32)
        parts.append(join_rows(product))
    gathered = jnp.concatenate(parts, axis=0)
    product = jnp.dot(split_rows(gathered), table[...], preferred_element_type=F32)
    return join_rows(product) * (SIDE_SCALE * scale)


def upper_kernel(side_ref, hidden_ref, wide_in, out_ref):
    out_ref[...] = widened(side_ref, hidden_ref, wide_in, (D / 3.0) ** (-0.5))


def feature_kernel(
    upper_ref,
    side_ref,
    query_ref,
    value_ref,
    wide_query,
    wide_value,
    scalar_ref,
    kept_ref,
    sent_ref,
):
    count = query_ref.shape[0]
    half = 2 * KR
    upper = upper_ref[...]
    query = widened(side_ref, query_ref, wide_query, (DQ / 3.0) ** (-0.5))
    value = widened(side_ref, value_ref, wide_value, (DV / 3.0) ** (-0.5))
    group = lax.rem(lax.broadcasted_iota(jnp.int32, query.shape, 0), half)
    lower = jnp.where(group < KR, query, value)
    targets = [scalar_ref[4 + item : 5 + item, 0:1] for item in range(count)]
    spots, pieces, slot_rows, width = kept_ref.shape
    place = lax.axis_index("dp")
    shard = lax.axis_index("fsdp")
    slots = slot_rows // KR
    first_half = lax.axis_index("rep") == 0
    per_block = KP // width
    zero = jnp.zeros((KR, KP), F32)
    for spot in range(spots):
        for block in range(4):
            source, at = (upper, lower)[block // 2], (block % 2) * KR
            wanted = []
            for slot in range(slots):
                total = zero
                for item in range(count):
                    rows_ = source[item * half + at : item * half + at + KR]
                    total = total + jnp.where(targets[item] == spot * slots + slot, rows_, 0.0)
                wanted.append(total)
            wanted = jnp.concatenate(wanted, axis=0)
            for chunk in range(block * per_block, (block + 1) * per_block, 2):
                at = (chunk % per_block) * width
                even, odd = wanted[:, at : at + width], wanted[:, at + width : at + 2 * width]
                kept_ref[spot ^ place, lax.rem(chunk // 2 + pieces - shard, pieces)] = jnp.where(first_half, even, odd)
                sent_ref[spot ^ place, lax.rem(chunk // 2 + pieces - shard, pieces)] = jnp.where(first_half, odd, even)


def finish_kernel(pieces_ref, out_ref):
    sources, _, width = pieces_ref.shape
    total = pieces_ref[0]
    for source in range(1, sources):
        total = total + pieces_ref[source]
    high = total.astype(BF16).astype(F32)
    rest = total - high
    middle = rest.astype(BF16).astype(F32)
    parts = jnp.concatenate([high, middle, rest - middle], axis=0).astype(BF16)
    row = lax.broadcasted_iota(jnp.int32, (width, width * KR), 0)
    col = lax.broadcasted_iota(jnp.int32, (width, width * KR), 1)
    spread = jnp.where(lax.shift_right_logical(col, 2) == row, 1.0, 0.0).astype(BF16)
    wide = jnp.dot(parts, spread, preferred_element_type=F32)
    count = total.shape[0]
    wide = wide[:count] + wide[count : 2 * count] + wide[2 * count :]
    rank = lax.broadcasted_iota(jnp.int32, wide.shape, 0) & (KR - 1)
    place = lax.broadcasted_iota(jnp.int32, wide.shape, 1) & (KR - 1)
    wide = jnp.where(rank == place, wide, 0.0)
    for slot in range(out_ref.shape[0]):
        out_ref[slot : slot + 1, :] = jnp.sum(
            wide[slot * KR : (slot + 1) * KR], axis=0, keepdims=True
        )


def in_vmem():
    return pl.BlockSpec(memory_space=pltpu.VMEM)


def in_hbm():
    return pl.BlockSpec(memory_space=pltpu.HBM)


def per_device(
    hidden_in,
    query_grad,
    value_grad,
    query_down,
    query_up,
    value_down,
    value_up,
    lengths,
    owners,
    proj_seed,
    offsets,
):
    count, rows, in_cols = hidden_in.shape
    q_cols = query_grad.shape[2]
    v_cols = value_grad.shape[2]
    shards = lax.axis_size("fsdp")
    spots = lax.axis_size("dp")
    upper, lower, scalars, hidden, query, value = pl.pallas_call(
        side_kernel,
        out_shape=(
            pltpu.VMEM((2 * KR, count * rows), F32),
            pltpu.VMEM((2 * KR, count * rows), F32),
            pltpu.VMEM((8, 128), jnp.int32),
            pltpu.VMEM(hidden_in.shape, BF16),
            pltpu.VMEM(query_grad.shape, BF16),
            pltpu.VMEM(value_grad.shape, BF16),
        ),
        in_specs=[in_hbm()] * 11,
        out_specs=[in_vmem()] * 6,
        scratch_shapes=[
            pltpu.VMEM(query_down.shape[::-1], BF16),
            pltpu.VMEM(query_up.shape, BF16),
            pltpu.VMEM(value_down.shape[::-1], BF16),
            pltpu.VMEM(value_up.shape, BF16),
            pltpu.SMEM(lengths.shape, jnp.int32),
            pltpu.SMEM(proj_seed.shape, jnp.int32),
            pltpu.SMEM(offsets.shape, jnp.int32),
            pltpu.SMEM(owners.shape, jnp.int32),
            pltpu.SemaphoreType.DMA((2, count, rows // BLOCK)),
            pltpu.SemaphoreType.DMA((2,)),
            pltpu.SemaphoreType.DMA((4,)),
        ],
        compiler_params=pltpu.CompilerParams(vmem_limit_bytes=42 * 2**20),
        name="sides",
    )(
        hidden_in,
        query_grad,
        value_grad,
        query_down.T,
        query_up,
        value_down.T,
        value_up,
        lengths,
        proj_seed,
        offsets,
        owners,
    )

    def make_tables(which, sizes):
        return pl.pallas_call(
            functools.partial(table_kernel, 32, which),
            out_shape=[pltpu.VMEM((size, KP), BF16) for size in sizes],
            in_specs=[in_vmem()],
            out_specs=[in_vmem()] * len(sizes),
            compiler_params=pltpu.CompilerParams(vmem_limit_bytes=16 * 2**20),
            name="tables",
        )(scalars)

    (wide_in,) = make_tables((0,), (in_cols,))
    wide_query, wide_value = make_tables((1, 2), (q_cols, v_cols))

    hop = 1
    while hop < shards:
        pairs = [(i, i ^ hop) for i in range(shards)]
        moved = lax.ppermute(upper, "fsdp", pairs)
        lower_moved = lax.ppermute(lower, "fsdp", pairs)
        if hop == 1:
            lower_moved, wide_in = lax.optimization_barrier((lower_moved, wide_in))
        upper = upper + moved
        lower = lower + lower_moved
        hop *= 2
    upper = pl.pallas_call(
        upper_kernel,
        out_shape=pltpu.VMEM((count * 2 * KR, KP), F32),
        in_specs=[in_vmem()] * 3,
        out_specs=in_vmem(),
        compiler_params=pltpu.CompilerParams(vmem_limit_bytes=16 * 2**20),
        name="upper",
    )(upper, hidden, wide_in)
    examples = owners.shape[0]
    slots = examples // spots
    width = 4 * KP // (2 * shards)
    kept, sent = pl.pallas_call(
        feature_kernel,
        out_shape=[pltpu.VMEM((spots, shards, slots * KR, width), F32)] * 2,
        in_specs=[in_vmem()] * 7,
        out_specs=[in_vmem()] * 2,
        compiler_params=pltpu.CompilerParams(vmem_limit_bytes=16 * 2**20),
        name="features",
    )(upper, lower, query, value, wide_query, wide_value, scalars)
    moved = []

    def add(value, axis, pairs):
        moved.append(lax.ppermute(value, axis, pairs))

    for hop in range(1, spots):
        crossed = [(2 * i + r, 2 * (i ^ hop) + 1 - r) for i in range(spots) for r in range(2)]
        add(sent[hop], ("dp", "rep"), crossed)
    add(sent[0], "rep", [(0, 1), (1, 0)])
    for hop in range(1, spots):
        add(kept[hop], "dp", [(i, i ^ hop) for i in range(spots)])
    mine = sum(moved, kept[0])
    parts = [mine[0]]
    for hop in range(shards - 1, 0, -1):
        pairs = [(i, (i + hop) % shards) for i in range(shards)]
        parts.append(lax.ppermute(mine[hop], "fsdp", pairs))
    parts = jnp.stack(parts)
    return pl.pallas_call(
        finish_kernel,
        out_shape=jax.ShapeDtypeStruct((slots, width * KR), F32),
        in_specs=[in_vmem()],
        out_specs=in_vmem(),
        compiler_params=pltpu.CompilerParams(vmem_limit_bytes=16 * 2**20),
        name="finish",
    )(parts)


def solution(mesh):
    placed = (
        P(("groups", "dp"), "rep", "fsdp"),
        P(("groups", "dp"), "rep", "fsdp"),
        P(("groups", "dp"), "rep", "fsdp"),
        P("fsdp", None),
        P(None, "fsdp"),
        P("fsdp", None),
        P(None, "fsdp"),
        P(("groups", "dp")),
        P("groups"),
        P(),
        P(),
    )
    return jax.shard_map(
        per_device,
        mesh=mesh,
        in_specs=placed,
        out_specs=P(("groups", "dp"), ("fsdp", "rep")),
        check_vma=False,
    )
```
